256 devices in a mesh: lat: 16 (over x, y_lo, core), lon: 16 (over z, y_hi).
Axes of the slice: x: 4, y: 4 (y_hi: 2, y_lo: 2; y = y_hi * 2 + y_lo), z: 8, core: 2. Of those that a mesh axis runs over, the one named last changes fastest.
Arguments:
- tokens: bfloat16 [4, 192, 384, 512], P(None, 'lat', 'lon'), may hold values from -6 to 6
- enc_gain: float32 [512], replicated, may hold values from 0.1 to 1.9
- enc_qkv: bfloat16 [512, 1536], P('lat', 'lon'), as said below
- enc_proj: bfloat16 [512, 512], P('lat', 'lon'), may hold values from -0.25 to 0.25
- merge_gain: float32 [2048], replicated, may hold values from 0.1 to 1.9
- merge_weight: bfloat16 [2048, 1024], P('lat', 'lon'), may hold values from -0.125 to 0.125
- split_weight: bfloat16 [1024, 2048], P('lat', 'lon'), may hold values from -0.1875 to 0.1875
- split_gain: float32 [512], replicated, may hold values from 0.1 to 1.9
- dec_gain: float32 [512], replicated, may hold values from 0.1 to 1.9
- dec_qkv: bfloat16 [512, 1536], P('lat', 'lon'), as said below
- dec_proj: bfloat16 [512, 512], P('lat', 'lon'), may hold values from -0.25 to 0.25
Outputs:
- decoded: bfloat16 [4, 192, 384, 512], P(None, 'lat', 'lon')
The draws below stay inside these ranges and needn't reach their ends.
Inputs may be any that keep to these rules, and one draw needn't show every extreme that they name: `enc_qkv`: a query, key and value projection of 8 heads. `dec_qkv`: a query, key and value projection of 8 heads.
All inputs are finite; a program needn't handle non-finite values.
Results may differ from the reference program's by a relative error of at most 0.04.
Values may be sent and summed in bfloat16 or wider, within the bound.
No kernel may reach another device: no remote copies, remote signals or barrier semaphores. Data moves between devices by JAX's collectives and lax.ppermute only.
A program may use at most 192 MiB of HBM per device.

```python
import jax
import jax.numpy as jnp
from jax import lax

C = 512
HEADS = 8
LEV = 4
WL = 2
WA = 6
WO = 12
NLAT = 192
NLON = 384


def aligned_qkv(key, low, high):
    first, second, third = jax.random.split(key, 3)
    base = jnp.clip(jax.random.normal(first, (C, 3 * C), jnp.float32), -4.0, 4.0) * C ** (-0.5)
    picked = jax.random.permutation(second, HEADS) < HEADS // 2
    boost = jax.random.uniform(third, (HEADS,), jnp.float32, low, high)
    factor = jnp.repeat(jnp.where(picked, boost, 1.0), C // HEADS)
    chosen = jnp.repeat(picked, C // HEADS)
    queries = base[:, :C] * factor
    keys_part = jnp.where(chosen[None, :], base[:, C:2 * C], base[:, C:2 * C])
    return jnp.concatenate([queries, keys_part, base[:, 2 * C:]], 1).astype(jnp.bfloat16)


def draw_enc_qkv(key, part):
    key = jax.random.fold_in(key, 11)
    return aligned_qkv(key, 1.0, 1.0)


def draw_dec_qkv(key, part):
    key = jax.random.fold_in(key, 23)
    return aligned_qkv(key, 1.0, 1.0)


def level_of(own_key, extent, shards, low, top_value):
    def one(dim, blocks):
        draws = jax.random.uniform(jax.random.fold_in(jax.random.fold_in(own_key, 6), dim), (blocks,), jnp.float32, low / len(shards), top_value / len(shards))
        return jnp.repeat(jnp.exp(draws), extent[dim] // blocks).reshape((-1,) + (1,) * (len(extent) - dim - 1))

    loudness = one(*shards[0])
    for cut in shards[1:]:
        loudness = loudness * one(*cut)
    return loudness


def scatter_about(key, shape, scale, limit, shards=(), dtype=jnp.bfloat16):
    result = jax.random.normal(key, shape, jnp.float32) * scale
    if len(shards) > 0:
        result = level_of(key, shape, shards, -0.22, 0.18) * result
    return jnp.clip(result, min=-limit, max=limit).astype(dtype)


def setup_inputs(seed: int = 0) -> dict:
    streams_of = jax.random.split(jax.random.key(seed), 12)
    tokens = scatter_about(streams_of[0], (LEV, NLAT, NLON, C), 1.0, 6.0, ((1, 16), (2, 16)))
    enc_gain = jnp.clip(1.0 + 0.18 * jax.random.normal(streams_of[1], (C,), jnp.float32), 0.1, 1.9)
    enc_qkv = draw_enc_qkv(jax.random.fold_in(streams_of[11], 71), 0)
    enc_proj = scatter_about(streams_of[3], (C, C), C ** -0.5, 0.25, ((0, 16), (1, 16)))
    merge_gain = jnp.clip(1.0 + 0.18 * jax.random.normal(streams_of[4], (4 * C,), jnp.float32), 0.1, 1.9)
    merge_weight = scatter_about(streams_of[5], (4 * C, 2 * C), (4 * C) ** -0.5, 0.125, ((0, 16), (1, 16)))
    split_weight = scatter_about(streams_of[6], (2 * C, 4 * C), (2 * C) ** -0.5, 0.1875, ((0, 16), (1, 16)))
    split_gain = jnp.clip(1.0 + 0.18 * jax.random.normal(streams_of[7], (C,), jnp.float32), 0.1, 1.9)
    dec_gain = jnp.clip(1.0 + 0.18 * jax.random.normal(streams_of[8], (C,), jnp.float32), 0.1, 1.9)
    dec_qkv = draw_dec_qkv(jax.random.fold_in(streams_of[11], 71), 0)
    dec_proj = scatter_about(streams_of[10], (C, C), C ** -0.5, 0.25, ((0, 16), (1, 16)))
    return dict(tokens=tokens, enc_gain=enc_gain, enc_qkv=enc_qkv, enc_proj=enc_proj, merge_gain=merge_gain, merge_weight=merge_weight, split_weight=split_weight, split_gain=split_gain, dec_gain=dec_gain, dec_qkv=dec_qkv, dec_proj=dec_proj)


eps = 1e-05

def layer_norm(values, gain):
    center = lax.optimization_barrier(jnp.mean(values, axis=-1, keepdims=True))
    centred = values - center
    spread = lax.optimization_barrier(jnp.mean(centred * centred, axis=-1, keepdims=True))
    return centred * lax.rsqrt(spread + eps) * gain

def region_labels(index, count, window):
    return (index >= count - window).astype(jnp.int32) + (index >= count - window // 2).astype(jnp.int32)

def attend(normed, qkv_weight, proj_weight, level_labels, lat_labels):
    levels, rows, cols, width = normed.shape
    head_dim = width // HEADS
    window_tokens = WL * WA * WO
    projected = jnp.dot(normed.reshape(-1, width), qkv_weight, preferred_element_type=jnp.float32).astype(jnp.bfloat16)
    projected = projected.reshape(levels // WL, WL, rows // WA, WA, cols // WO, WO, 3, HEADS, head_dim)
    projected = projected.transpose(0, 2, 4, 6, 7, 1, 3, 5, 8).reshape(-1, 3, HEADS, window_tokens, head_dim)
    labels = level_labels.astype(jnp.int32)[:, None, None] * 3 + lat_labels.astype(jnp.int32)[None, :, None] + jnp.zeros((1, 1, cols), jnp.int32)
    labels = labels.reshape(levels // WL, WL, rows // WA, WA, cols // WO, WO).transpose(0, 2, 4, 1, 3, 5).reshape(-1, window_tokens)
    queries = projected[:, 0].astype(jnp.float32)
    keys_part = projected[:, 1].astype(jnp.float32)
    values_part = projected[:, 2].astype(jnp.float32)
    scores = jnp.einsum('nhqd,nhkd->nhqk', queries, keys_part) * head_dim ** (-0.5)
    same = labels[:, None, :, None] == labels[:, None, None, :]
    scores = jnp.where(same, scores, -jnp.inf)
    weights = jax.nn.softmax(scores, axis=-1).astype(jnp.bfloat16)
    mixed = jnp.einsum('nhqk,nhkd->nhqd', weights.astype(jnp.float32), values_part).astype(jnp.bfloat16)
    mixed = mixed.reshape(levels // WL, rows // WA, cols // WO, HEADS, WL, WA, WO, head_dim)
    mixed = mixed.transpose(0, 4, 1, 5, 2, 6, 3, 7).reshape(-1, width)
    output = jnp.dot(mixed, proj_weight, preferred_element_type=jnp.float32).astype(jnp.bfloat16)
    return output.reshape(levels, rows, cols, width)

def decode_band(band, merge_gain, merge_weight, split_weight, split_gain, dec_gain, dec_qkv, dec_proj):
    levels, rows, cols, width = band.shape
    quads = jnp.concatenate([band[:, 0::2, 0::2], band[:, 1::2, 0::2], band[:, 0::2, 1::2], band[:, 1::2, 1::2]], -1)
    merged_normed = layer_norm(quads.astype(jnp.float32), merge_gain).astype(jnp.bfloat16)
    middle = jnp.dot(merged_normed.reshape(-1, 4 * width), merge_weight, preferred_element_type=jnp.float32).astype(jnp.bfloat16)
    split_out = jnp.dot(middle, split_weight, preferred_element_type=jnp.float32)
    split_out = split_out.reshape(levels, rows // 2, cols // 2, 2, 2, width).transpose(0, 1, 3, 2, 4, 5).reshape(levels, rows, cols, width)
    joined = (layer_norm(split_out, split_gain) + band.astype(jnp.float32)).astype(jnp.bfloat16)
    dec_normed = layer_norm(joined.astype(jnp.float32), dec_gain).astype(jnp.bfloat16)
    dec_branch = attend(dec_normed, dec_qkv, dec_proj, jnp.zeros((levels,), jnp.int32), jnp.zeros((rows,), jnp.int32))
    return (joined.astype(jnp.float32) + dec_branch.astype(jnp.float32)).astype(jnp.bfloat16)

def reference(tokens, enc_gain, enc_qkv, enc_proj, merge_gain, merge_weight, split_weight, split_gain, dec_gain, dec_qkv, dec_proj):
    bands = NLAT // WA
    enc_normed = layer_norm(tokens.astype(jnp.float32), enc_gain).astype(jnp.bfloat16)
    shifted = jnp.roll(enc_normed, (-(WL // 2), -(WA // 2), -(WO // 2)), axis=(0, 1, 2))
    level_labels = region_labels(jnp.arange(LEV), LEV, WL)
    lat_labels = region_labels(jnp.arange(NLAT), NLAT, WA)
    banded = shifted.reshape(LEV, bands, WA, NLON, C).transpose(1, 0, 2, 3, 4)

    def encode_band(pair):
        return attend(pair[0], enc_qkv, enc_proj, level_labels, pair[1])
    branch = lax.map(encode_band, (banded, lat_labels.reshape(bands, WA)))
    branch = branch.transpose(1, 0, 2, 3, 4).reshape(LEV, NLAT, NLON, C)
    branch = jnp.roll(branch, (WL // 2, WA // 2, WO // 2), axis=(0, 1, 2))
    encoded = (tokens.astype(jnp.float32) + branch.astype(jnp.float32)).astype(jnp.bfloat16)
    enc_bands = encoded.reshape(LEV, bands, WA, NLON, C).transpose(1, 0, 2, 3, 4)

    def decode_one(band):
        return decode_band(band, merge_gain, merge_weight, split_weight, split_gain, dec_gain, dec_qkv, dec_proj)
    decoded = lax.map(decode_one, enc_bands)
    return decoded.transpose(1, 0, 2, 3, 4).reshape(LEV, NLAT, NLON, C)
```

```python
import functools

import jax
import jax.numpy as jnp
import numpy as np
from jax import lax
from jax.experimental import pallas as pl
from jax.experimental.pallas import tpu as pltpu
from jax.sharding import PartitionSpec as P

HEADS = 8
WL = 2
WA = 6
WO = 12
WIN = WL * WA * WO
C = 512
HD = C // HEADS
LEV = 4
ROWS = 12
COLS = 24
BAND = 2 * WIN
VMEM_LIMIT = 48 * 1024 * 1024

eps = 1e-05
SCALE = float(HD**-0.5 * np.log2(np.e))


def window_from_natural():
    out = np.zeros((BAND, BAND), np.float32)
    for l in range(WL):
        for r in range(WA):
            for c in range(COLS):
                out[(c // WO) * WIN + (l * WA + r) * WO + c % WO, (l * WA + r) * COLS + c] = 1
    return out


def merged_from_natural():
    out = np.zeros((BAND, BAND), np.float32)
    quarter = BAND // 4
    for l in range(WL):
        for r in range(WA):
            for c in range(COLS):
                part = (c % 2) * 2 + r % 2
                out[part * quarter + (l * (WA // 2) + r // 2) * (COLS // 2) + c // 2, (l * WA + r) * COLS + c] = 1
    return out


MERGE_PART = [0, 2, 1, 3]


def normed(values, gain):
    center = jnp.mean(values, axis=-1, keepdims=True)
    centred = values - center
    spread = jnp.mean(centred * centred, axis=-1, keepdims=True)
    return centred * lax.rsqrt(spread + eps) * gain


def dot(a, b):
    return jnp.dot(a, b, preferred_element_type=jnp.float32)


def window_attention(qkv_ref, mixed_ref, first, same):
    lane = lax.broadcasted_iota(jnp.int32, (WIN, 2 * HD), 1)
    low = lane < HD
    rows = pl.ds(first, WIN)
    for pair in range(HEADS // 2):
        at = pair * 2 * HD
        q = qkv_ref[rows, at : at + 2 * HD]
        k = qkv_ref[rows, C + at : C + at + 2 * HD]
        v = qkv_ref[rows, 2 * C + at : 2 * C + at + 2 * HD]
        vo = jnp.concatenate([v, jnp.ones_like(v)], axis=1)
        halves = []
        for half in range(2):
            own = low if half == 0 else ~low
            scores = lax.dot_general(
                jnp.where(own, q, jnp.zeros_like(q)), k, (((1,), (1,)), ((), ())), preferred_element_type=jnp.float32
            )
            scores = scores * SCALE
            if same is not None:
                scores = jnp.where(same, scores, -jnp.inf)
            top = jnp.max(scores, axis=-1, keepdims=True)
            weights = jnp.exp2(scores - top).astype(jnp.bfloat16)
            summed = dot(weights, vo)
            halves.append(summed[:, : 2 * HD] / summed[:, 2 * HD :])
        mixed_ref[rows, at : at + 2 * HD] = jnp.where(low, halves[0], halves[1]).astype(jnp.bfloat16)


def encode_kernel(last_ref, x_ref, gain_ref, w_ref, to_win_ref, from_win_ref, out_ref, qkv_ref, mixed_ref):
    step = pl.program_id(0)
    pair, band = step // 2, step % 2
    upper, lower = 2 * pair + 1, (2 * pair + 2) % LEV
    x = jnp.concatenate([x_ref[upper, band], x_ref[lower, band]], axis=0).astype(jnp.float32)
    h = normed(x, gain_ref[...]).astype(jnp.bfloat16)
    h = dot(to_win_ref[...], h).astype(jnp.bfloat16)
    for third in range(3):
        qkv_ref[:, third * C : (third + 1) * C] = dot(h, w_ref[:, third].reshape(C, C)).astype(jnp.bfloat16)
    by_level = (pair == 1).astype(jnp.int32)
    by_row = jnp.where(band == 1, last_ref[0], 0)

    def label(dim):
        index = lax.broadcasted_iota(jnp.int32, (WIN, WIN), dim)
        second = (index >= WIN // 2).astype(jnp.int32)
        inner = index - second * (WIN // 2)
        return by_level * 3 * second + by_row * (inner >= WIN // 4).astype(jnp.int32)

    same = label(0) == label(1)
    for window in range(2):
        window_attention(qkv_ref, mixed_ref, window * WIN, same)
    y = dot(mixed_ref[...], w_ref[:, 3].reshape(C, C)).astype(jnp.bfloat16)
    y = dot(from_win_ref[...], y)
    out = (x + y).astype(jnp.bfloat16)
    out_ref[upper, band] = out[:WIN]
    out_ref[lower, band] = out[WIN:]


def merge_split_kernel(x_ref, mgain_ref, sgain_ref, wm_ref, ws_ref, to_merged_ref, out_ref, quads_ref, skip_ref, middle_ref):
    step = pl.program_id(0)
    quarter = BAND // 4

    @pl.when(step == 0)
    def _():
        for pair in range(2):
            for band in range(2):
                x = jnp.concatenate([x_ref[2 * pair, band], x_ref[2 * pair + 1, band]], axis=0)
                m = dot(to_merged_ref[...], x)
                at = (pair * 2 + band) * quarter
                for part in range(4):
                    skip_ref[part, at : at + quarter] = m[part * quarter : (part + 1) * quarter]
        parts = [skip_ref[part] for part in range(4)]
        center = sum(jnp.sum(p, axis=-1, keepdims=True) for p in parts) * (1 / (4 * C))
        spread = sum(jnp.sum((p - center) * (p - center), axis=-1, keepdims=True) for p in parts) * (1 / (4 * C))
        scale = lax.rsqrt(spread + eps)
        for part in range(4):
            quads_ref[:, part * C : (part + 1) * C] = (
                (parts[part] - center) * scale * mgain_ref[:, part * C : (part + 1) * C]
            ).astype(jnp.bfloat16)

    @pl.when(step < 4)
    def _():
        width = wm_ref.shape[-1]
        middle_ref[step] = dot(quads_ref[...], wm_ref[:, 0].reshape(4 * C, width)).astype(jnp.bfloat16)

    @pl.when(step >= 4)
    def _():
        part = step - 4
        width = middle_ref.shape[-1]
        w = ws_ref[:, 0].reshape(2 * C, C)
        total = dot(middle_ref[0], w[:width])
        for chunk in range(1, 4):
            total += dot(middle_ref[chunk], w[chunk * width : (chunk + 1) * width])
        kept = (part % 2) * 2 + part // 2
        joined = (normed(total, sgain_ref[...]) + skip_ref[kept]).astype(jnp.bfloat16)
        out_ref[0] = joined


def decode_kernel(x_ref, gain_ref, w_ref, to_win_ref, from_win_ref, out_ref, qkv_ref, mixed_ref):
    step = pl.program_id(0)
    pair, band = step // 2, step % 2
    quarter = BAND // 4
    x = jnp.concatenate([x_ref[part, step].astype(jnp.float32) for part in range(4)], axis=0).astype(jnp.bfloat16)
    x = dot(to_win_ref[...], x)
    h = normed(x, gain_ref[...]).astype(jnp.bfloat16)
    for third in range(3):
        qkv_ref[:, third * C : (third + 1) * C] = dot(h, w_ref[:, third].reshape(C, C)).astype(jnp.bfloat16)
    for window in range(2):
        window_attention(qkv_ref, mixed_ref, window * WIN, None)
    y = dot(mixed_ref[...], w_ref[:, 3].reshape(C, C)).astype(jnp.bfloat16)
    out = (x + y.astype(jnp.float32)).astype(jnp.bfloat16)
    out = dot(from_win_ref[...], out).astype(jnp.bfloat16)
    out_ref[2 * pair, band] = out[:WIN]
    out_ref[2 * pair + 1, band] = out[WIN:]


def whole(shape):
    return pl.BlockSpec(shape, lambda i: (0,) * len(shape))


PARAMS = pltpu.CompilerParams(vmem_limit_bytes=VMEM_LIMIT)


def encode(framed, gain, weights, last):
    to_win = window_from_natural()
    shape = (LEV, 2, WIN, C)
    return pl.pallas_call(
        encode_kernel,
        grid=(4,),
        in_specs=[
            pl.BlockSpec(memory_space=pltpu.SMEM),
            whole(shape),
            whole((1, C)),
            whole((16, 4, 32, C)),
            whole((BAND, BAND)),
            whole((BAND, BAND)),
        ],
        out_specs=whole(shape),
        out_shape=jax.ShapeDtypeStruct(shape, jnp.bfloat16),
        scratch_shapes=[pltpu.VMEM((BAND, 3 * C), jnp.bfloat16), pltpu.VMEM((BAND, C), jnp.bfloat16)],
        compiler_params=PARAMS,
        name="encode",
    )(last, framed, gain.reshape(1, C), weights, jnp.asarray(to_win, jnp.bfloat16), jnp.asarray(to_win.T, jnp.bfloat16))


def merge_split(encoded, mgain, sgain, weights):
    to_merged = merged_from_natural()
    tokens = LEV * ROWS * COLS // 4
    return pl.pallas_call(
        merge_split_kernel,
        grid=(8,),
        in_specs=[
            whole((LEV, 2, WIN, C)),
            whole((1, 4 * C)),
            whole((1, C)),
            pl.BlockSpec((16, 1, 128, 256), lambda i: (0, jnp.minimum(i, 3) // 2, 0, jnp.minimum(i, 3) % 2)),
            pl.BlockSpec((16, 1, 64, C), lambda i: (0, jnp.maximum(i, 4), 0, 0)),
            whole((BAND, BAND)),
        ],
        out_specs=pl.BlockSpec(
            (1, tokens, C),
            lambda i: ((jnp.maximum(i - 4, 0) % 2) * 2 + jnp.maximum(i - 4, 0) // 2, 0, 0),
        ),
        out_shape=jax.ShapeDtypeStruct((4, tokens, C), jnp.bfloat16),
        scratch_shapes=[
            pltpu.VMEM((tokens, 4 * C), jnp.bfloat16),
            pltpu.VMEM((4, tokens, C), jnp.float32),
            pltpu.VMEM((4, tokens, 256), jnp.bfloat16),
        ],
        compiler_params=PARAMS,
        name="merge_split",
    )(
        encoded,
        mgain.reshape(1, 4 * C),
        sgain.reshape(1, C),
        weights.reshape(16, 4, 128, C),
        weights.reshape(16, 8, 64, C),
        jnp.asarray(to_merged, jnp.bfloat16),
    )


def decode(joined, gain, weights):
    to_win = window_from_natural()
    from_merged = to_win @ merged_from_natural().T
    shape = (LEV, 2, WIN, C)
    return pl.pallas_call(
        decode_kernel,
        grid=(4,),
        in_specs=[
            whole((4, 4, BAND // 4, C)),
            whole((1, C)),
            whole((16, 4, 32, C)),
            whole((BAND, BAND)),
            whole((BAND, BAND)),
        ],
        out_specs=whole(shape),
        out_shape=jax.ShapeDtypeStruct(shape, jnp.bfloat16),
        scratch_shapes=[pltpu.VMEM((BAND, 3 * C), jnp.bfloat16), pltpu.VMEM((BAND, C), jnp.bfloat16)],
        compiler_params=PARAMS,
        name="decode",
    )(
        joined.reshape(4, 4, BAND // 4, C),
        gain.reshape(1, C),
        weights,
        jnp.asarray(from_merged, jnp.bfloat16),
        jnp.asarray(to_win.T, jnp.bfloat16),
    )


def passed_along(value, axis, steps):
    if isinstance(axis, str):
        count = lax.axis_size(axis)
        pairs = [(source, (source + steps) % count) for source in range(count)]
    else:
        rows, cols = (lax.axis_size(name) for name in axis)
        pairs = [
            (i * cols + j, ((i + steps) % rows) * cols + (j + steps) % cols) for i in range(rows) for j in range(cols)
        ]
    return lax.ppermute(value, axis, pairs)


def gathered_cols(block):
    return lax.all_to_all(jnp.broadcast_to(block[None], (16,) + block.shape), "lon", 0, 0, tiled=True)


def pack_attention(qkv, proj):
    return jnp.concatenate([qkv, proj], axis=1)


def unpack_attention(blocks):
    qkv = blocks[:, :, :96].transpose(1, 0, 2).reshape(32, 3, C).transpose(1, 0, 2)
    proj = blocks[:, :, 96:].transpose(1, 0, 2).reshape(1, 32, C)
    return jnp.concatenate([qkv, proj], axis=0)


def shards(
    tokens,
    enc_gain,
    enc_qkv,
    enc_proj,
    merge_gain,
    merge_weight,
    split_weight,
    split_gain,
    dec_gain,
    dec_qkv,
    dec_proj,
):
    half_lat = WA // 2
    half_lon = WO // 2
    packed = jnp.concatenate(
        [
            pack_attention(enc_qkv, enc_proj),
            pack_attention(dec_qkv, dec_proj),
            jnp.concatenate([merge_weight[:64], merge_weight[64:]], axis=1),
            split_weight,
        ],
        axis=0,
    )
    blocks = gathered_cols(packed)
    enc_rows = unpack_attention(blocks[:, :32])
    dec_rows = unpack_attention(blocks[:, 32:64])
    merge_rows = (
        blocks[:, 64:128].reshape(16, 64, 2, 64).transpose(2, 1, 0, 3).reshape(128, 2, C).transpose(1, 0, 2)
    )
    split_rows = blocks[:, 128:].transpose(1, 0, 2).reshape(64, 4, C).transpose(1, 0, 2)
    enc_w = lax.all_gather(enc_rows, "lat", axis=0, tiled=False)
    ms_rows = jnp.concatenate([merge_rows.reshape(256, C), split_rows.reshape(256, C)], axis=0)
    ms_w = lax.all_gather(ms_rows, "lat", axis=0, tiled=False)
    dec_w = lax.all_gather(dec_rows, "lat", axis=0, tiled=False)

    below = passed_along(tokens[:, :half_lat, half_lon:], "lat", -1)
    beyond = passed_along(tokens[:, half_lat:, :half_lon], "lon", -1)
    corner = passed_along(tokens[:, :half_lat, :half_lon], ("lat", "lon"), -1)
    framed = jnp.concatenate(
        [
            jnp.concatenate([tokens[:, half_lat:, half_lon:], beyond], axis=2),
            jnp.concatenate([below, corner], axis=2),
        ],
        axis=1,
    )
    last = (lax.axis_index("lat") == lax.axis_size("lat") - 1).astype(jnp.int32).reshape(1)
    moved = encode(framed.reshape(LEV, 2, WIN, C), enc_gain, enc_w, last).reshape(LEV, ROWS, COLS, C)
    cut_r, cut_c = ROWS - half_lat, COLS - half_lon
    above = passed_along(moved[:, cut_r:, :cut_c], "lat", 1)
    left = passed_along(moved[:, :cut_r, cut_c:], "lon", 1)
    corner = passed_along(moved[:, cut_r:, cut_c:], ("lat", "lon"), 1)
    encoded = jnp.concatenate(
        [
            jnp.concatenate([corner, above], axis=2),
            jnp.concatenate([left, moved[:, :cut_r, :cut_c]], axis=2),
        ],
        axis=1,
    )
    joined = merge_split(encoded.reshape(LEV, 2, WIN, C), merge_gain, split_gain, ms_w)
    return decode(joined, dec_gain, dec_w).reshape(LEV, ROWS, COLS, C)


def solution(mesh):
    return jax.shard_map(
        shards,
        mesh=mesh,
        in_specs=(
            P(None, "lat", "lon", None),
            P(),
            P("lat", "lon"),
            P("lat", "lon"),
            P(),
            P("lat", "lon"),
            P("lat", "lon"),
            P(),
            P(),
            P("lat", "lon"),
            P("lat", "lon"),
        ),
        out_specs=P(None, "lat", "lon", None),
        check_vma=False,
    )
```

```python
import functools

import jax
import jax.numpy as jnp
import numpy as np
from jax import lax
from jax.experimental import pallas as pl
from jax.experimental.pallas import tpu as pltpu
from jax.sharding import PartitionSpec as P

HEADS = 8
WL = 2
WA = 6
WO = 12
WIN = WL * WA * WO
C = 512
HD = C // HEADS
LEV = 4
ROWS = 12
COLS = 24
BAND = 2 * WIN
VMEM_LIMIT = 48 * 1024 * 1024

eps = 1e-05
SCALE = float(HD**-0.5 * np.log2(np.e))


def window_from_natural():
    out = np.zeros((BAND, BAND), np.float32)
    for l in range(WL):
        for r in range(WA):
            for c in range(COLS):
                out[(c // WO) * WIN + (l * WA + r) * WO + c % WO, (l * WA + r) * COLS + c] = 1
    return out


def merged_from_natural():
    out = np.zeros((BAND, BAND), np.float32)
    quarter = BAND // 4
    for l in range(WL):
        for r in range(WA):
            for c in range(COLS):
                part = (c % 2) * 2 + r % 2
                out[part * quarter + (l * (WA // 2) + r // 2) * (COLS // 2) + c // 2, (l * WA + r) * COLS + c] = 1
    return out


MERGE_PART = [0, 2, 1, 3]


def normed(values, gain):
    center = jnp.mean(values, axis=-1, keepdims=True)
    centred = values - center
    spread = jnp.mean(centred * centred, axis=-1, keepdims=True)
    return centred * lax.rsqrt(spread + eps) * gain


def dot(a, b):
    return jnp.dot(a, b, preferred_element_type=jnp.float32)


def window_attention(qkv_ref, mixed_ref, first, same):
    lane = lax.broadcasted_iota(jnp.int32, (WIN, 2 * HD), 1)
    low = lane < HD
    rows = pl.ds(first, WIN)
    for pair in range(HEADS // 2):
        at = pair * 2 * HD
        q = qkv_ref[rows, at : at + 2 * HD]
        k = qkv_ref[rows, C + at : C + at + 2 * HD]
        v = qkv_ref[rows, 2 * C + at : 2 * C + at + 2 * HD]
        vo = jnp.concatenate([v, jnp.ones_like(v)], axis=1)
        halves = []
        for half in range(2):
            own = low if half == 0 else ~low
            scores = lax.dot_general(
                jnp.where(own, q, jnp.zeros_like(q)), k, (((1,), (1,)), ((), ())), preferred_element_type=jnp.float32
            )
            scores = scores * SCALE
            if same is not None:
                scores = jnp.where(same, scores, -jnp.inf)
            top = jnp.max(scores, axis=-1, keepdims=True)
            weights = jnp.exp2(scores - top).astype(jnp.bfloat16)
            summed = dot(weights, vo)
            halves.append(summed[:, : 2 * HD] / summed[:, 2 * HD :])
        mixed_ref[rows, at : at + 2 * HD] = jnp.where(low, halves[0], halves[1]).astype(jnp.bfloat16)


def put_attention(w_ref, rows, group, blocks):
    w_ref[rows, group * 384 : (group + 1) * 384] = jnp.concatenate([b[:, :96] for b in blocks], axis=1)
    w_ref[rows, 3 * C + group * 128 : 3 * C + (group + 1) * 128] = jnp.concatenate([b[:, 96:] for b in blocks], axis=1)


def slots_of(place_ref, x, yl):
    px, py = place_ref[0], place_ref[1]
    return lax.rem(px - x + 4, 4), [lax.rem(py - (2 * yh + yl) + 4, 4) for yh in range(2)]


def unpack_encoder(place_ref, raws, w_ref):
    px, py, pz, me = (place_ref[i] for i in range(4))
    for side in range(2):
        near, far = raws[2 * side], raws[2 * side + 1]
        core = lax.rem(me + side, 2)
        for slot in range(4):
            x = lax.rem(px - slot + 4, 4)
            raw = near if slot == 0 else far.at[slot - 1]
            for yl in range(2):
                _, ys = slots_of(place_ref, 0, yl)
                rows = pl.ds(pl.multiple_of((x * 4 + yl * 2 + core) * 32, 32), 32)
                for group in range(4):
                    blocks = [raw[ys[j % 2], lax.rem(2 * group + j // 2 - pz + 12, 8)] for j in range(4)]
                    put_attention(w_ref, rows, group, blocks)


def unpack_decoder(place_ref, raw_ref, w_ref):
    for x in range(4):
        for yl in range(2):
            sx, ys = slots_of(place_ref, x, yl)
            for core in range(2):
                first = (x * 4 + yl * 2 + core) * 32
                for group in range(4):
                    blocks = [raw_ref[2 * group + j // 2, core, sx, ys[j % 2]] for j in range(4)]
                    put_attention(w_ref, slice(first, first + 32), group, blocks)


def encode_kernel(place_ref, x_ref, gain_ref, r0, r1, r2, r3, to_win_ref, from_win_ref, out_ref, w_ref, qkv_ref, mixed_ref):
    step = pl.program_id(0)

    @pl.when(step == 0)
    def _():
        unpack_encoder(place_ref, (r0, r1, r2, r3), w_ref)

    pair, band = step // 2, step % 2
    upper, lower = 2 * pair + 1, (2 * pair + 2) % LEV
    x = jnp.concatenate([x_ref[upper, band], x_ref[lower, band]], axis=0).astype(jnp.float32)
    h = normed(x, gain_ref[...]).astype(jnp.bfloat16)
    h = dot(to_win_ref[...], h).astype(jnp.bfloat16)
    for third in range(3):
        qkv_ref[:, third * C : (third + 1) * C] = dot(h, w_ref[:, third * C : (third + 1) * C]).astype(jnp.bfloat16)
    by_level = (pair == 1).astype(jnp.int32)
    by_row = jnp.where(band == 1, place_ref[4], 0)

    def label(dim):
        index = lax.broadcasted_iota(jnp.int32, (WIN, WIN), dim)
        second = (index >= WIN // 2).astype(jnp.int32)
        inner = index - second * (WIN // 2)
        return by_level * 3 * second + by_row * (inner >= WIN // 4).astype(jnp.int32)

    same = label(0) == label(1)
    for window in range(2):
        window_attention(qkv_ref, mixed_ref, window * WIN, same)
    y = dot(mixed_ref[...], w_ref[:, 3 * C :]).astype(jnp.bfloat16)
    y = dot(from_win_ref[...], y)
    out = (x + y).astype(jnp.bfloat16)
    out_ref[upper, band] = out[:WIN]
    out_ref[lower, band] = out[WIN:]


def merge_split_kernel(
    place_ref, x_ref, mgain_ref, sgain_ref, wm_ref, ws_ref, to_merged_ref, out_ref, quads_ref, skip_ref, middle_ref, w_ref, w2_ref
):
    step = pl.program_id(0)
    quarter = BAND // 4

    @pl.when(step == 0)
    def _():
        for pair in range(2):
            for band in range(2):
                x = jnp.concatenate([x_ref[2 * pair, band], x_ref[2 * pair + 1, band]], axis=0)
                m = dot(to_merged_ref[...], x)
                at = (pair * 2 + band) * quarter
                for part in range(4):
                    skip_ref[part, at : at + quarter] = m[part * quarter : (part + 1) * quarter]
        parts = [skip_ref[part] for part in range(4)]
        center = sum(jnp.sum(p, axis=-1, keepdims=True) for p in parts) * (1 / (4 * C))
        spread = sum(jnp.sum((p - center) * (p - center), axis=-1, keepdims=True) for p in parts) * (1 / (4 * C))
        scale = lax.rsqrt(spread + eps)
        for part in range(4):
            quads_ref[:, part * C : (part + 1) * C] = (
                (parts[part] - center) * scale * mgain_ref[:, part * C : (part + 1) * C]
            ).astype(jnp.bfloat16)

    @pl.when(step < 4)
    def _():
        for x in range(4):
            for yl in range(2):
                sx, ys = slots_of(place_ref, x, yl)
                for core in range(2):
                    first = (x * 4 + yl * 2 + core) * 128
                    for z in range(2):
                        left, right = (wm_ref[z, core, sx, y] for y in ys)
                        cols = slice(z * 128, (z + 1) * 128)
                        w_ref[first : first + 64, cols] = jnp.concatenate([left[:, :64], right[:, :64]], axis=1)
                        w_ref[first + 64 : first + 128, cols] = jnp.concatenate([left[:, 64:], right[:, 64:]], axis=1)
        middle_ref[step] = dot(quads_ref[...], w_ref[...]).astype(jnp.bfloat16)

    @pl.when(step >= 4)
    def _():
        part = step - 4
        width = middle_ref.shape[-1]
        for x in range(4):
            for yl in range(2):
                sx, ys = slots_of(place_ref, x, yl)
                for core in range(2):
                    first = (x * 4 + yl * 2 + core) * 64
                    for z in range(2):
                        for yh in range(2):
                            lon = 2 * z + yh
                            w2_ref[first : first + 64, lon * 128 : (lon + 1) * 128] = ws_ref[z, core, sx, ys[yh]]
        total = dot(middle_ref[0], w2_ref[:width])
        for chunk in range(1, 4):
            total += dot(middle_ref[chunk], w2_ref[chunk * width : (chunk + 1) * width])
        kept = (part % 2) * 2 + part // 2
        joined = (normed(total, sgain_ref[...]) + skip_ref[kept]).astype(jnp.bfloat16)
        out_ref[0] = joined


def decode_kernel(place_ref, x_ref, gain_ref, raw_ref, to_win_ref, from_win_ref, out_ref, w_ref, qkv_ref, mixed_ref):
    step = pl.program_id(0)

    @pl.when(step == 0)
    def _():
        unpack_decoder(place_ref, raw_ref, w_ref)


    pair, band = step // 2, step % 2
    quarter = BAND // 4
    x = jnp.concatenate([x_ref[part, step].astype(jnp.float32) for part in range(4)], axis=0).astype(jnp.bfloat16)
    x = dot(to_win_ref[...], x)
    h = normed(x, gain_ref[...]).astype(jnp.bfloat16)
    for third in range(3):
        qkv_ref[:, third * C : (third + 1) * C] = dot(h, w_ref[:, third * C : (third + 1) * C]).astype(jnp.bfloat16)
    for window in range(2):
        window_attention(qkv_ref, mixed_ref, window * WIN, None)
    y = dot(mixed_ref[...], w_ref[:, 3 * C :]).astype(jnp.bfloat16)
    out = (x + y.astype(jnp.float32)).astype(jnp.bfloat16)
    out = dot(from_win_ref[...], out).astype(jnp.bfloat16)
    out_ref[2 * pair, band] = out[:WIN]
    out_ref[2 * pair + 1, band] = out[WIN:]


def whole(shape):
    return pl.BlockSpec(shape, lambda i: (0,) * len(shape))


PARAMS = pltpu.CompilerParams(vmem_limit_bytes=VMEM_LIMIT)


def encode(framed, gain, weights, place):
    to_win = window_from_natural()
    shape = (LEV, 2, WIN, C)
    return pl.pallas_call(
        encode_kernel,
        grid=(4,),
        in_specs=[
            pl.BlockSpec(memory_space=pltpu.SMEM),
            whole(shape),
            whole((1, C)),
            *[whole(raw.shape) for raw in weights],
            whole((BAND, BAND)),
            whole((BAND, BAND)),
        ],
        out_specs=whole(shape),
        out_shape=jax.ShapeDtypeStruct(shape, jnp.bfloat16),
        scratch_shapes=[
            pltpu.VMEM((C, 4 * C), jnp.bfloat16),
            pltpu.VMEM((BAND, 3 * C), jnp.bfloat16),
            pltpu.VMEM((BAND, C), jnp.bfloat16),
        ],
        compiler_params=PARAMS,
        name="encode",
    )(place, framed, gain.reshape(1, C), *weights, jnp.asarray(to_win, jnp.bfloat16), jnp.asarray(to_win.T, jnp.bfloat16))


def merge_split(encoded, mgain, sgain, raw, place):
    to_merged = merged_from_natural()
    tokens = LEV * ROWS * COLS // 4
    return pl.pallas_call(
        merge_split_kernel,
        grid=(8,),
        in_specs=[
            pl.BlockSpec(memory_space=pltpu.SMEM),
            whole((LEV, 2, WIN, C)),
            whole((1, 4 * C)),
            whole((1, C)),
            pl.BlockSpec((2, 2, 4, 4, 64, 128), lambda i: (jnp.minimum(i, 3), 0, 0, 0, 0, 0)),
            pl.BlockSpec((2, 2, 4, 4, 64, 128), lambda i: (jnp.maximum(i - 4, 0), 0, 0, 0, 1, 0)),
            whole((BAND, BAND)),
        ],
        out_specs=pl.BlockSpec(
            (1, tokens, C),
            lambda i: ((jnp.maximum(i - 4, 0) % 2) * 2 + jnp.maximum(i - 4, 0) // 2, 0, 0),
        ),
        out_shape=jax.ShapeDtypeStruct((4, tokens, C), jnp.bfloat16),
        scratch_shapes=[
            pltpu.VMEM((tokens, 4 * C), jnp.bfloat16),
            pltpu.VMEM((4, tokens, C), jnp.float32),
            pltpu.VMEM((4, tokens, 256), jnp.bfloat16),
            pltpu.VMEM((4 * C, 256), jnp.bfloat16),
            pltpu.VMEM((2 * C, C), jnp.bfloat16),
        ],
        compiler_params=PARAMS,
        name="merge_split",
    )(
        place,
        encoded,
        mgain.reshape(1, 4 * C),
        sgain.reshape(1, C),
        raw,
        raw,
        jnp.asarray(to_merged, jnp.bfloat16),
    )


def decode(joined, gain, weights, place):
    to_win = window_from_natural()
    from_merged = to_win @ merged_from_natural().T
    shape = (LEV, 2, WIN, C)
    return pl.pallas_call(
        decode_kernel,
        grid=(4,),
        in_specs=[
            pl.BlockSpec(memory_space=pltpu.SMEM),
            whole((4, 4, BAND // 4, C)),
            whole((1, C)),
            pl.BlockSpec((8, 2, 4, 4, 32, 128), lambda i: (0, 0, 0, 0, 4, 0)),
            whole((BAND, BAND)),
            whole((BAND, BAND)),
        ],
        out_specs=whole(shape),
        out_shape=jax.ShapeDtypeStruct(shape, jnp.bfloat16),
        scratch_shapes=[
            pltpu.VMEM((C, 4 * C), jnp.bfloat16),
            pltpu.VMEM((BAND, 3 * C), jnp.bfloat16),
            pltpu.VMEM((BAND, C), jnp.bfloat16),
        ],
        compiler_params=PARAMS,
        name="decode",
    )(
        place,
        joined.reshape(4, 4, BAND // 4, C),
        gain.reshape(1, C),
        weights,
        jnp.asarray(from_merged, jnp.bfloat16),
        jnp.asarray(to_win.T, jnp.bfloat16),
    )


def passed_along(value, axis, steps):
    if isinstance(axis, str):
        count = lax.axis_size(axis)
        pairs = [(source, (source + steps) % count) for source in range(count)]
    else:
        rows, cols = (lax.axis_size(name) for name in axis)
        pairs = [
            (i * cols + j, ((i + steps) % rows) * cols + (j + steps) % cols) for i in range(rows) for j in range(cols)
        ]
    return lax.ppermute(value, axis, pairs)


def device_index(x, y, z, core):
    return (x * 4 + (y % 2) * 2 + core) * 16 + z * 2 + y // 2


def chips():
    return [(x, y, z, core) for x in range(4) for y in range(4) for z in range(8) for core in range(2)]


def sent(value, to):
    return lax.ppermute(value, ("lat", "lon"), [(device_index(*at), device_index(*to(*at))) for at in chips()])


def from_x(value):
    return [sent(value, lambda x, y, z, c: ((x + steps) % 4, y, z, c)) for steps in (1, 2, 3)]


def from_y(value):
    return [sent(value, lambda x, y, z, c: (x, (y + steps) % 4, z, c)) for steps in (1, 2, 3)]


def from_z(value, steps):
    return sent(value, lambda x, y, z, c: (x, y, (z + steps) % 8, c))


def z_and_cores(value):
    groups = [
        [device_index(x, y, z, core) for z in range(8) for core in range(2)] for x in range(4) for y in range(4)
    ]
    return lax.all_gather(value, ("lat", "lon"), axis=0, tiled=False, axis_index_groups=groups)


def other_core(value):
    return sent(value, lambda x, y, z, c: (x, y, z, 1 - c))


def together(*values):
    return lax.optimization_barrier(values)


def shards(
    tokens,
    enc_gain,
    enc_qkv,
    enc_proj,
    merge_gain,
    merge_weight,
    split_weight,
    split_gain,
    dec_gain,
    dec_qkv,
    dec_proj,
):
    half_lat = WA // 2
    half_lon = WO // 2
    lat, lon = lax.axis_index("lat"), lax.axis_index("lon")
    last = lat == lax.axis_size("lat") - 1
    place = jnp.stack([lat // 4, (lon % 2) * 2 + (lat // 2) % 2, lon // 2, lat % 2, last.astype(jnp.int32)]).astype(jnp.int32)
    enc_share = jnp.concatenate([enc_qkv, enc_proj], axis=1)
    later_share = jnp.concatenate(
        [
            jnp.concatenate([merge_weight[:64], merge_weight[64:]], axis=1),
            split_weight,
            jnp.concatenate([dec_qkv, dec_proj], axis=1),
        ],
        axis=0,
    )

    later_y = from_y(later_share)
    enc_near = [from_z(enc_share, 1), from_z(enc_share, -1)]
    later_near = jnp.stack([later_share, *later_y])
    later_x = from_x(later_near)
    enc_three = jnp.stack([enc_near[0], enc_share, enc_near[1]])
    enc_far = [from_z(enc_three, 3), from_z(enc_three[:2], -3)]
    tokens_sent, later_x = together(tokens, later_x)
    later_raw = z_and_cores(jnp.stack([later_near, *later_x])).reshape(8, 2, 4, 4, 160, 128)
    below = passed_along(tokens_sent[:, :half_lat, half_lon:], "lat", -1)
    beyond = passed_along(tokens_sent[:, half_lat:, :half_lon], "lon", -1)
    corner = passed_along(tokens_sent[:, :half_lat, :half_lon], ("lat", "lon"), -1)
    enc_far, below, beyond, corner = together(enc_far, below, beyond, corner)
    enc_z = jnp.concatenate([enc_far[0], enc_three, enc_far[1]], axis=0)
    enc_y = jnp.stack([enc_z, *from_y(enc_z)])
    enc_x = jnp.stack(from_x(enc_y))
    enc_raw = [enc_y, enc_x, other_core(enc_y), other_core(enc_x)]
    framed = jnp.concatenate(
        [
            jnp.concatenate([tokens[:, half_lat:, half_lon:], beyond], axis=2),
            jnp.concatenate([below, corner], axis=2),
        ],
        axis=1,
    )
    moved = encode(framed.reshape(LEV, 2, WIN, C), enc_gain, enc_raw, place).reshape(LEV, ROWS, COLS, C)
    cut_r, cut_c = ROWS - half_lat, COLS - half_lon
    above = passed_along(moved[:, cut_r:, :cut_c], "lat", 1)
    left = passed_along(moved[:, :cut_r, cut_c:], "lon", 1)
    corner = passed_along(moved[:, cut_r:, cut_c:], ("lat", "lon"), 1)
    encoded = jnp.concatenate(
        [
            jnp.concatenate([corner, above], axis=2),
            jnp.concatenate([left, moved[:, :cut_r, :cut_c]], axis=2),
        ],
        axis=1,
    )
    joined = merge_split(encoded.reshape(LEV, 2, WIN, C), merge_gain, split_gain, later_raw, place)
    return decode(joined, dec_gain, later_raw, place).reshape(LEV, ROWS, COLS, C)


def solution(mesh):
    return jax.shard_map(
        shards,
        mesh=mesh,
        in_specs=(
            P(None, "lat", "lon", None),
            P(),
            P("lat", "lon"),
            P("lat", "lon"),
            P(),
            P("lat", "lon"),
            P("lat", "lon"),
            P(),
            P(),
            P("lat", "lon"),
            P("lat", "lon"),
        ),
        out_specs=P(None, "lat", "lon", None),
        check_vma=False,
    )
```

```python
import functools

import jax
import jax.numpy as jnp
import numpy as np
from jax import lax
from jax.experimental import pallas as pl
from jax.experimental.pallas import tpu as pltpu
from jax.sharding import PartitionSpec as P

HEADS = 8
WL = 2
WA = 6
WO = 12
WIN = WL * WA * WO
C = 512
HD = C // HEADS
LEV = 4
ROWS = 12
COLS = 24
BAND = 2 * WIN
VMEM_LIMIT = 48 * 1024 * 1024

eps = 1e-05
SCALE = float(HD**-0.5 * np.log2(np.e))


def window_from_natural():
    out = np.zeros((BAND, BAND), np.float32)
    for l in range(WL):
        for r in range(WA):
            for c in range(COLS):
                out[(c // WO) * WIN + (l * WA + r) * WO + c % WO, (l * WA + r) * COLS + c] = 1
    return out


def level_windows():
    return window_from_natural().reshape(2, WL, WIN // 2, WL, WIN)[:, 0, :, 0].reshape(WIN, WIN)


def merged_from_natural():
    out = np.zeros((BAND, BAND), np.float32)
    quarter = BAND // 4
    for l in range(WL):
        for r in range(WA):
            for c in range(COLS):
                part = (c % 2) * 2 + r % 2
                out[part * quarter + (l * (WA // 2) + r // 2) * (COLS // 2) + c // 2, (l * WA + r) * COLS + c] = 1
    return out


MERGE_PART = [0, 2, 1, 3]


def normed(values, gain):
    center = jnp.mean(values, axis=-1, keepdims=True)
    centred = values - center
    spread = jnp.mean(centred * centred, axis=-1, keepdims=True)
    return centred * lax.rsqrt(spread + eps) * gain


def dot(a, b):
    return jnp.dot(a, b, preferred_element_type=jnp.float32)


def window_attention(qkv_ref, mixed_ref, first, same):
    lane = lax.broadcasted_iota(jnp.int32, (WIN, 2 * HD), 1)
    low = lane < HD
    rows = pl.ds(first, WIN)
    for pair in range(HEADS // 2):
        at = pair * 2 * HD
        q = qkv_ref[rows, at : at + 2 * HD]
        k = qkv_ref[rows, C + at : C + at + 2 * HD]
        v = qkv_ref[rows, 2 * C + at : 2 * C + at + 2 * HD]
        vo = jnp.concatenate([v, jnp.ones_like(v)], axis=1)
        halves = []
        for half in range(2):
            own = low if half == 0 else ~low
            scores = lax.dot_general(
                jnp.where(own, q, jnp.zeros_like(q)), k, (((1,), (1,)), ((), ())), preferred_element_type=jnp.float32
            )
            scores = scores * SCALE
            if same is not None:
                scores = jnp.where(same, scores, -jnp.inf)
            top = jnp.max(scores, axis=-1, keepdims=True)
            weights = jnp.exp2(scores - top).astype(jnp.bfloat16)
            summed = dot(weights, vo)
            halves.append(summed[:, : 2 * HD] / summed[:, 2 * HD :])
        mixed_ref[rows, at : at + 2 * HD] = jnp.where(low, halves[0], halves[1]).astype(jnp.bfloat16)


def put_attention(w_ref, rows, group, blocks):
    w_ref[rows, group * 384 : (group + 1) * 384] = jnp.concatenate([b[:, :96] for b in blocks], axis=1)
    w_ref[rows, 3 * C + group * 128 : 3 * C + (group + 1) * 128] = jnp.concatenate([b[:, 96:] for b in blocks], axis=1)


def unpack_encoder(place_ref, raws, w_ref):
    px, py, pz, me = (place_ref[i] for i in range(4))
    for side in range(2):
        near, far = raws[2 * side], raws[2 * side + 1]
        core = lax.rem(me + side, 2)
        for slot in range(4):
            x = lax.rem(px - slot + 4, 4)
            raw = near if slot == 0 else far.at[slot - 1]
            for yl in range(2):
                ys = [lax.rem(py - (2 * yh + yl) + 4, 4) for yh in range(2)]
                rows = pl.ds(pl.multiple_of((x * 4 + yl * 2 + core) * 32, 32), 32)
                for group in range(4):
                    blocks = [raw[ys[j % 2], lax.rem(2 * group + j // 2 - pz + 12, 8)] for j in range(4)]
                    put_attention(w_ref, rows, group, blocks)


def unpack_decoder(raw_ref, w_ref, x):
    for yl in range(2):
        sx, ys = x, (yl, 2 + yl)
        for core in range(2):
            rows = pl.ds(pl.multiple_of((x * 4 + yl * 2 + core) * 32, 32), 32)
            for group in range(4):
                blocks = [raw_ref[2 * group + j // 2, core, sx, ys[j % 2]] for j in range(4)]
                put_attention(w_ref, rows, group, blocks)


def to_windows(level_ref, first, second):
    first, second = dot(level_ref[...], first), dot(level_ref[...], second)
    half = WIN // 2
    return jnp.concatenate([first[:half], second[:half], first[half:], second[half:]], axis=0)


def from_windows(level_ref, values):
    half = WIN // 2
    first = jnp.concatenate([values[:half], values[WIN : WIN + half]], axis=0).astype(jnp.bfloat16)
    second = jnp.concatenate([values[half:WIN], values[WIN + half :]], axis=0).astype(jnp.bfloat16)
    return dot(level_ref[...], first), dot(level_ref[...], second)


def encode_kernel(band, place_ref, x_ref, gain_ref, to_win_ref, from_win_ref, *refs):
    pair = pl.program_id(0)
    if band == 1:
        *raws, out_ref, w_ref, qkv_ref, mixed_ref = refs

        @pl.when(pair == 0)
        def _():
            unpack_encoder(place_ref, raws, w_ref)
    else:
        w_ref, out_ref, qkv_ref, mixed_ref = refs

    upper, lower = 2 * pair + 1, (2 * pair + 2) % LEV
    x = [x_ref[level].astype(jnp.float32) for level in (upper, lower)]
    h = [normed(level, gain_ref[...]).astype(jnp.bfloat16) for level in x]
    h = to_windows(to_win_ref, *h).astype(jnp.bfloat16)
    for third in range(3):
        qkv_ref[:, third * C : (third + 1) * C] = dot(h, w_ref[:, third * C : (third + 1) * C]).astype(jnp.bfloat16)
    by_level = (pair == 1).astype(jnp.int32)
    by_row = place_ref[4] if band == 1 else 0

    def label(dim):
        index = lax.broadcasted_iota(jnp.int32, (WIN, WIN), dim)
        second = (index >= WIN // 2).astype(jnp.int32)
        inner = index - second * (WIN // 2)
        return by_level * 3 * second + by_row * (inner >= WIN // 4).astype(jnp.int32)

    same = label(0) == label(1)
    for window in range(2):
        window_attention(qkv_ref, mixed_ref, window * WIN, same)
    y = from_windows(from_win_ref, dot(mixed_ref[...], w_ref[:, 3 * C :]))
    out_ref[upper] = (x[0] + y[0]).astype(jnp.bfloat16)
    out_ref[lower] = (x[1] + y[1]).astype(jnp.bfloat16)


def merge_split_kernel(
    x_ref,
    mgain_ref,
    sgain_ref,
    wm_ref,
    ws_ref,
    wd_ref,
    to_merged_ref,
    out_ref,
    dec_ref,
    quads_ref,
    skip_ref,
    middle_ref,
    w_ref,
    w2_ref,
):
    step = pl.program_id(0)
    quarter = BAND // 4

    @pl.when(step == 0)
    def _():
        for pair in range(2):
            for band in range(2):
                x = jnp.concatenate([x_ref[2 * pair, band], x_ref[2 * pair + 1, band]], axis=0)
                m = dot(to_merged_ref[...], x)
                at = (pair * 2 + band) * quarter
                for part in range(4):
                    skip_ref[part, at : at + quarter] = m[part * quarter : (part + 1) * quarter]
        parts = [skip_ref[part] for part in range(4)]
        center = sum(jnp.sum(p, axis=-1, keepdims=True) for p in parts) * (1 / (4 * C))
        spread = sum(jnp.sum((p - center) * (p - center), axis=-1, keepdims=True) for p in parts) * (1 / (4 * C))
        scale = lax.rsqrt(spread + eps)
        for part in range(4):
            quads_ref[:, part * C : (part + 1) * C] = (
                (parts[part] - center) * scale * mgain_ref[:, part * C : (part + 1) * C]
            ).astype(jnp.bfloat16)

    @pl.when(step < 4)
    def _():
        for x in range(4):
            for yl in range(2):
                sx, ys = x, (yl, 2 + yl)
                for core in range(2):
                    first = (x * 4 + yl * 2 + core) * 128
                    for z in range(2):
                        left, right = (wm_ref[z, core, sx, y] for y in ys)
                        cols = slice(z * 128, (z + 1) * 128)
                        w_ref[first : first + 64, cols] = jnp.concatenate([left[:, :64], right[:, :64]], axis=1)
                        w_ref[first + 64 : first + 128, cols] = jnp.concatenate([left[:, 64:], right[:, 64:]], axis=1)
        middle_ref[step] = dot(quads_ref[...], w_ref[...]).astype(jnp.bfloat16)

    @pl.when(step >= 4)
    def _():
        part = step - 4
        width = middle_ref.shape[-1]
        for x in range(4):
            for yl in range(2):
                sx, ys = x, (yl, 2 + yl)
                for core in range(2):
                    first = (x * 4 + yl * 2 + core) * 64
                    for z in range(2):
                        for yh in range(2):
                            lon = 2 * z + yh
                            w2_ref[first : first + 64, lon * 128 : (lon + 1) * 128] = ws_ref[z, core, sx, ys[yh]]
        total = dot(middle_ref[0], w2_ref[:width])
        for chunk in range(1, 4):
            total += dot(middle_ref[chunk], w2_ref[chunk * width : (chunk + 1) * width])
        unpack_decoder(wd_ref, dec_ref, part)
        kept = (part % 2) * 2 + part // 2
        joined = (normed(total, sgain_ref[...]) + skip_ref[kept]).astype(jnp.bfloat16)
        out_ref[0] = joined


def decode_kernel(x_ref, gain_ref, w_ref, to_win_ref, from_win_ref, out_ref, qkv_ref, mixed_ref):
    step = pl.program_id(0)
    pair, band = step // 2, step % 2
    quarter = BAND // 4
    x = jnp.concatenate([x_ref[part, step].astype(jnp.float32) for part in range(4)], axis=0).astype(jnp.bfloat16)
    x = dot(to_win_ref[...], x)
    h = normed(x, gain_ref[...]).astype(jnp.bfloat16)
    for third in range(3):
        qkv_ref[:, third * C : (third + 1) * C] = dot(h, w_ref[:, third * C : (third + 1) * C]).astype(jnp.bfloat16)
    for window in range(2):
        window_attention(qkv_ref, mixed_ref, window * WIN, None)
    y = dot(mixed_ref[...], w_ref[:, 3 * C :]).astype(jnp.bfloat16)
    first, second = from_windows(from_win_ref, x + y.astype(jnp.float32))
    out_ref[2 * pair, band] = first.astype(jnp.bfloat16)
    out_ref[2 * pair + 1, band] = second.astype(jnp.bfloat16)


def whole(shape):
    return pl.BlockSpec(shape, lambda i: (0,) * len(shape))


PARAMS = pltpu.CompilerParams(vmem_limit_bytes=VMEM_LIMIT)


def encode(band, framed, gain, weights, place):
    to_win = level_windows()
    shape = (LEV, WIN, C)
    out_shapes, out_specs = [jax.ShapeDtypeStruct(shape, jnp.bfloat16)], [whole(shape)]
    if band == 1:
        out_shapes.append(jax.ShapeDtypeStruct((C, 4 * C), jnp.bfloat16))
        out_specs.append(whole((C, 4 * C)))
    return pl.pallas_call(
        functools.partial(encode_kernel, band),
        grid=(2,),
        in_specs=[
            pl.BlockSpec(memory_space=pltpu.SMEM),
            whole(shape),
            whole((1, C)),
            whole((WIN, WIN)),
            whole((WIN, WIN)),
            *[whole(raw.shape) for raw in weights],
        ],
        out_specs=out_specs,
        out_shape=out_shapes,
        scratch_shapes=[pltpu.VMEM((BAND, 3 * C), jnp.bfloat16), pltpu.VMEM((BAND, C), jnp.bfloat16)],
        compiler_params=PARAMS,
        cost_estimate=pl.CostEstimate(flops=2 * 10**9, bytes_accessed=4 * 10**6, transcendentals=700_000),
        name=f"encode_band{band}",
    )(
        place,
        framed.reshape(shape),
        gain.reshape(1, C),
        jnp.asarray(to_win, jnp.bfloat16),
        jnp.asarray(to_win.T, jnp.bfloat16),
        *weights,
    )


def merge_split(encoded, mgain, sgain, raw):
    to_merged = merged_from_natural()
    tokens = LEV * ROWS * COLS // 4
    return pl.pallas_call(
        merge_split_kernel,
        grid=(8,),
        in_specs=[
            whole((LEV, 2, WIN, C)),
            whole((1, 4 * C)),
            whole((1, C)),
            pl.BlockSpec((2, 2, 4, 4, 64, 128), lambda i: (jnp.minimum(i, 3), 0, 0, 0, 0, 0)),
            pl.BlockSpec((2, 2, 4, 4, 64, 128), lambda i: (jnp.maximum(i - 4, 0), 0, 0, 0, 1, 0)),
            pl.BlockSpec((8, 2, 4, 4, 32, 128), lambda i: (0, 0, 0, 0, 4, 0)),
            whole((BAND, BAND)),
        ],
        out_specs=[
            pl.BlockSpec(
                (1, tokens, C),
                lambda i: ((jnp.maximum(i - 4, 0) % 2) * 2 + jnp.maximum(i - 4, 0) // 2, 0, 0),
            ),
            whole((C, 4 * C)),
        ],
        out_shape=[
            jax.ShapeDtypeStruct((4, tokens, C), jnp.bfloat16),
            jax.ShapeDtypeStruct((C, 4 * C), jnp.bfloat16),
        ],
        scratch_shapes=[
            pltpu.VMEM((tokens, 4 * C), jnp.bfloat16),
            pltpu.VMEM((4, tokens, C), jnp.float32),
            pltpu.VMEM((4, tokens, 256), jnp.bfloat16),
            pltpu.VMEM((4 * C, 256), jnp.bfloat16),
            pltpu.VMEM((2 * C, C), jnp.bfloat16),
        ],
        compiler_params=PARAMS,
        name="merge_split",
    )(
        encoded,
        mgain.reshape(1, 4 * C),
        sgain.reshape(1, C),
        raw,
        raw,
        raw,
        jnp.asarray(to_merged, jnp.bfloat16),
    )


def decode(joined, gain, weights):
    to_win = window_from_natural()
    from_merged = to_win @ merged_from_natural().T
    shape = (LEV, 2, WIN, C)
    return pl.pallas_call(
        decode_kernel,
        grid=(4,),
        in_specs=[
            whole((4, 4, BAND // 4, C)),
            whole((1, C)),
            whole((C, 4 * C)),
            whole((BAND, BAND)),
            whole((WIN, WIN)),
        ],
        out_specs=whole(shape),
        out_shape=jax.ShapeDtypeStruct(shape, jnp.bfloat16),
        scratch_shapes=[
            pltpu.VMEM((BAND, 3 * C), jnp.bfloat16),
            pltpu.VMEM((BAND, C), jnp.bfloat16),
        ],
        compiler_params=PARAMS,
        name="decode",
    )(
        joined.reshape(4, 4, BAND // 4, C),
        gain.reshape(1, C),
        weights,
        jnp.asarray(from_merged, jnp.bfloat16),
        jnp.asarray(level_windows().T, jnp.bfloat16),
    )


def passed_along(value, axis, steps):
    if isinstance(axis, str):
        count = lax.axis_size(axis)
        pairs = [(source, (source + steps) % count) for source in range(count)]
    else:
        rows, cols = (lax.axis_size(name) for name in axis)
        pairs = [
            (i * cols + j, ((i + steps) % rows) * cols + (j + steps) % cols) for i in range(rows) for j in range(cols)
        ]
    return lax.ppermute(value, axis, pairs)


def device_index(x, y, z, core):
    return (x * 4 + (y % 2) * 2 + core) * 16 + z * 2 + y // 2


def chips():
    return [(x, y, z, core) for x in range(4) for y in range(4) for z in range(8) for core in range(2)]


def sent(value, to):
    return lax.ppermute(value, ("lat", "lon"), [(device_index(*at), device_index(*to(*at))) for at in chips()])


def from_x(value):
    return [sent(value, lambda x, y, z, c: ((x + steps) % 4, y, z, c)) for steps in (1, 2, 3)]


def from_y(value):
    return [sent(value, lambda x, y, z, c: (x, (y + steps) % 4, z, c)) for steps in (1, 2, 3)]


def from_z(value, steps):
    return sent(value, lambda x, y, z, c: (x, y, (z + steps) % 8, c))


def x_and_y(value):
    groups = [
        [device_index(x, y, z, core) for x in range(4) for y in range(4)] for z in range(8) for core in range(2)
    ]
    blocks = jnp.broadcast_to(value[None], (16,) + value.shape)
    blocks = lax.all_to_all(blocks, ("lat", "lon"), 0, 0, tiled=True, axis_index_groups=groups)
    return blocks.reshape((4, 4) + value.shape)


def z_and_cores(value):
    groups = [
        [device_index(x, y, z, core) for z in range(8) for core in range(2)] for x in range(4) for y in range(4)
    ]
    return lax.all_gather(value, ("lat", "lon"), axis=0, tiled=False, axis_index_groups=groups)


def other_core(value):
    return sent(value, lambda x, y, z, c: (x, y, z, 1 - c))


def together(*values):
    return lax.optimization_barrier(values)


def shards(
    tokens,
    enc_gain,
    enc_qkv,
    enc_proj,
    merge_gain,
    merge_weight,
    split_weight,
    split_gain,
    dec_gain,
    dec_qkv,
    dec_proj,
):
    half_lat = WA // 2
    half_lon = WO // 2
    lat, lon = lax.axis_index("lat"), lax.axis_index("lon")
    last = lat == lax.axis_size("lat") - 1
    place = jnp.stack([lat // 4, (lon % 2) * 2 + (lat // 2) % 2, lon // 2, lat % 2, last.astype(jnp.int32)]).astype(jnp.int32)
    enc_share = jnp.concatenate([enc_qkv, enc_proj], axis=1)
    later_share = jnp.concatenate(
        [
            jnp.concatenate([merge_weight[:64], merge_weight[64:]], axis=1),
            split_weight,
            jnp.concatenate([dec_qkv, dec_proj], axis=1),
        ],
        axis=0,
    )

    later = x_and_y(later_share)
    enc_near = [from_z(enc_share, 1), from_z(enc_share, -1)]
    enc_three = jnp.stack([enc_near[0], enc_share, enc_near[1]])
    tokens_sent, enc_three = together(tokens[:, :half_lat], enc_three)
    enc_far, below, later = together(
        [from_z(enc_three, 3), from_z(enc_three[:2], -3)], passed_along(tokens_sent, "lat", -1), later
    )
    later_raw = z_and_cores(later).reshape(8, 2, 4, 4, 160, 128)
    enc_z = jnp.concatenate([enc_far[0], enc_three, enc_far[1]], axis=0)
    edge = jnp.concatenate([tokens[:, half_lat:, :half_lon], below[:, :, :half_lon]], axis=1)
    enc_y, beyond = together(from_y(enc_z), passed_along(edge, "lon", -1))
    enc_y = jnp.stack([enc_z, *enc_y])
    enc_x = jnp.stack(from_x(enc_y))
    enc_raw = [enc_y, enc_x, other_core(enc_y), other_core(enc_x)]
    framed = jnp.concatenate(
        [jnp.concatenate([tokens[:, half_lat + WA :], below], axis=1)[:, :, half_lon:], beyond[:, WA:]], axis=2
    )
    second, enc_w = encode(1, framed, enc_gain, enc_raw, place)
    second = second.reshape(LEV, WA, COLS, C)
    above = passed_along(second[:, WA - half_lat :], "lat", 1)
    framed = jnp.concatenate([tokens[:, half_lat : half_lat + WA, half_lon:], beyond[:, :WA]], axis=2)
    (first,) = encode(0, framed, enc_gain, [enc_w], place)
    first = first.reshape(LEV, WA, COLS, C)
    rows = jnp.concatenate([above, first, second[:, : WA - half_lat]], axis=1)
    left = passed_along(rows[:, :, COLS - half_lon :], "lon", 1)
    encoded = jnp.concatenate([left, rows[:, :, : COLS - half_lon]], axis=2)
    joined, dec_w = merge_split(encoded.reshape(LEV, 2, WIN, C), merge_gain, split_gain, later_raw)
    return decode(joined, dec_gain, dec_w).reshape(LEV, ROWS, COLS, C)


def solution(mesh):
    return jax.shard_map(
        shards,
        mesh=mesh,
        in_specs=(
            P(None, "lat", "lon", None),
            P(),
            P("lat", "lon"),
            P("lat", "lon"),
            P(),
            P("lat", "lon"),
            P("lat", "lon"),
            P(),
            P(),
            P("lat", "lon"),
            P("lat", "lon"),
        ),
        out_specs=P(None, "lat", "lon", None),
        check_vma=False,
    )
```

```python
import functools

import jax
import jax.numpy as jnp
import numpy as np
from jax import lax
from jax.experimental import pallas as pl
from jax.experimental.pallas import tpu as pltpu
from jax.sharding import PartitionSpec as P

HEADS = 8
WL = 2
WA = 6
WO = 12
WIN = WL * WA * WO
C = 512
HD = C // HEADS
LEV = 4
ROWS = 12
COLS = 24
BAND = 2 * WIN
VMEM_LIMIT = 48 * 1024 * 1024

eps = 1e-05
SCALE = float(HD**-0.5 * np.log2(np.e))


def window_from_natural():
    out = np.zeros((BAND, BAND), np.float32)
    for l in range(WL):
        for r in range(WA):
            for c in range(COLS):
                out[(c // WO) * WIN + (l * WA + r) * WO + c % WO, (l * WA + r) * COLS + c] = 1
    return out


def level_windows():
    return window_from_natural().reshape(2, WL, WIN // 2, WL, WIN)[:, 0, :, 0].reshape(WIN, WIN)


def merged_from_natural():
    out = np.zeros((BAND, BAND), np.float32)
    quarter = BAND // 4
    for l in range(WL):
        for r in range(WA):
            for c in range(COLS):
                part = (c % 2) * 2 + r % 2
                out[part * quarter + (l * (WA // 2) + r // 2) * (COLS // 2) + c // 2, (l * WA + r) * COLS + c] = 1
    return out


MERGE_PART = [0, 2, 1, 3]


def normed(values, gain):
    center = jnp.mean(values, axis=-1, keepdims=True)
    centred = values - center
    spread = jnp.mean(centred * centred, axis=-1, keepdims=True)
    return centred * lax.rsqrt(spread + eps) * gain


def dot(a, b):
    return jnp.dot(a, b, preferred_element_type=jnp.float32)


def window_attention(qkv_ref, mixed_ref, first, same):
    lane = lax.broadcasted_iota(jnp.int32, (WIN, 2 * HD), 1)
    low = lane < HD
    rows = pl.ds(first, WIN)
    for pair in range(HEADS // 2):
        at = pair * 2 * HD
        q = qkv_ref[rows, at : at + 2 * HD]
        k = qkv_ref[rows, C + at : C + at + 2 * HD]
        v = qkv_ref[rows, 2 * C + at : 2 * C + at + 2 * HD]
        vo = jnp.concatenate([v, jnp.ones_like(v)], axis=1)
        halves = []
        for half in range(2):
            own = low if half == 0 else ~low
            scores = lax.dot_general(
                jnp.where(own, q, jnp.zeros_like(q)), k, (((1,), (1,)), ((), ())), preferred_element_type=jnp.float32
            )
            scores = scores * SCALE
            if same is not None:
                scores = jnp.where(same, scores, -jnp.inf)
            top = jnp.max(scores, axis=-1, keepdims=True)
            weights = jnp.exp2(scores - top).astype(jnp.bfloat16)
            summed = dot(weights, vo)
            halves.append(summed[:, : 2 * HD] / summed[:, 2 * HD :])
        mixed_ref[rows, at : at + 2 * HD] = jnp.where(low, halves[0], halves[1]).astype(jnp.bfloat16)


def put_attention(w_ref, rows, group, blocks):
    w_ref[rows, group * 384 : (group + 1) * 384] = jnp.concatenate([b[:, :96] for b in blocks], axis=1)
    w_ref[rows, 3 * C + group * 128 : 3 * C + (group + 1) * 128] = jnp.concatenate([b[:, 96:] for b in blocks], axis=1)


def unpack_encoder(place_ref, raws, w_ref):
    px, py, pz, me = (place_ref[i] for i in range(4))
    for side in range(2):
        near, far = raws[2 * side], raws[2 * side + 1]
        core = lax.rem(me + side, 2)
        for slot in range(4):
            x = lax.rem(px - slot + 4, 4)
            raw = near if slot == 0 else far.at[slot - 1]
            for yl in range(2):
                ys = [lax.rem(py - (2 * yh + yl) + 4, 4) for yh in range(2)]
                rows = pl.ds(pl.multiple_of((x * 4 + yl * 2 + core) * 32, 32), 32)
                for group in range(4):
                    blocks = [raw[ys[j % 2], lax.rem(2 * group + j // 2 - pz + 12, 8)] for j in range(4)]
                    put_attention(w_ref, rows, group, blocks)


def unpack_decoder(place_ref, raws, w_ref, slot):
    px, py, pz, me = (place_ref[i] for i in range(4))
    x = lax.rem(px - slot + 4, 4)
    for side in range(2):
        core = lax.rem(me + side, 2)
        for yl in range(2):
            ys = [lax.rem(py - (2 * yh + yl) + 4, 4) for yh in range(2)]
            rows = pl.ds(pl.multiple_of((x * 4 + yl * 2 + core) * 32, 32), 32)
            for group in range(4):
                blocks = [raws[side][0, ys[j % 2], lax.rem(2 * group + j // 2 - pz + 12, 8)] for j in range(4)]
                put_attention(w_ref, rows, group, blocks)


def to_windows(level_ref, first, second):
    first, second = dot(level_ref[...], first), dot(level_ref[...], second)
    half = WIN // 2
    return jnp.concatenate([first[:half], second[:half], first[half:], second[half:]], axis=0)


def from_windows(level_ref, values):
    half = WIN // 2
    first = jnp.concatenate([values[:half], values[WIN : WIN + half]], axis=0).astype(jnp.bfloat16)
    second = jnp.concatenate([values[half:WIN], values[WIN + half :]], axis=0).astype(jnp.bfloat16)
    return dot(level_ref[...], first), dot(level_ref[...], second)


def encode_kernel(band, place_ref, x_ref, gain_ref, to_win_ref, from_win_ref, *refs):
    pair = pl.program_id(0)
    if band == 1:
        *raws, out_ref, w_ref, qkv_ref, mixed_ref = refs

        @pl.when(pair == 0)
        def _():
            unpack_encoder(place_ref, raws, w_ref)
    else:
        w_ref, out_ref, qkv_ref, mixed_ref = refs

    upper, lower = 2 * pair + 1, (2 * pair + 2) % LEV
    x = [x_ref[level].astype(jnp.float32) for level in (upper, lower)]
    h = [normed(level, gain_ref[...]).astype(jnp.bfloat16) for level in x]
    h = to_windows(to_win_ref, *h).astype(jnp.bfloat16)
    for third in range(3):
        qkv_ref[:, third * C : (third + 1) * C] = dot(h, w_ref[:, third * C : (third + 1) * C]).astype(jnp.bfloat16)
    by_level = (pair == 1).astype(jnp.int32)
    by_row = place_ref[4] if band == 1 else 0

    def label(dim):
        index = lax.broadcasted_iota(jnp.int32, (WIN, WIN), dim)
        second = (index >= WIN // 2).astype(jnp.int32)
        inner = index - second * (WIN // 2)
        return by_level * 3 * second + by_row * (inner >= WIN // 4).astype(jnp.int32)

    same = label(0) == label(1)
    for window in range(2):
        window_attention(qkv_ref, mixed_ref, window * WIN, same)
    y = from_windows(from_win_ref, dot(mixed_ref[...], w_ref[:, 3 * C :]))
    out_ref[upper] = (x[0] + y[0]).astype(jnp.bfloat16)
    out_ref[lower] = (x[1] + y[1]).astype(jnp.bfloat16)


def merge_split_kernel(
    place_ref,
    x_ref,
    mgain_ref,
    sgain_ref,
    raw_ref,
    own_ref,
    other_ref,
    to_merged_ref,
    out_ref,
    dec_ref,
    quads_ref,
    skip_ref,
    middle_ref,
    w_ref,
    w2_ref,
):
    step = pl.program_id(0)
    quarter = BAND // 4

    @pl.when(step == 0)
    def _():
        for pair in range(2):
            for band in range(2):
                x = jnp.concatenate([x_ref[2 * pair, band], x_ref[2 * pair + 1, band]], axis=0)
                m = dot(to_merged_ref[...], x)
                at = (pair * 2 + band) * quarter
                for part in range(4):
                    skip_ref[part, at : at + quarter] = m[part * quarter : (part + 1) * quarter]
        parts = [skip_ref[part] for part in range(4)]
        center = sum(jnp.sum(p, axis=-1, keepdims=True) for p in parts) * (1 / (4 * C))
        spread = sum(jnp.sum((p - center) * (p - center), axis=-1, keepdims=True) for p in parts) * (1 / (4 * C))
        scale = lax.rsqrt(spread + eps)
        for part in range(4):
            quads_ref[:, part * C : (part + 1) * C] = (
                (parts[part] - center) * scale * mgain_ref[:, part * C : (part + 1) * C]
            ).astype(jnp.bfloat16)

    @pl.when(step < 4)
    def _():
        for x in range(4):
            for yl in range(2):
                sx, ys = x, (yl, 2 + yl)
                for core in range(2):
                    first = (x * 4 + yl * 2 + core) * 128
                    for z in range(2):
                        left, right = (raw_ref[z, core, sx, y] for y in ys)
                        cols = slice(z * 128, (z + 1) * 128)
                        w_ref[first : first + 64, cols] = jnp.concatenate([left[:, :64], right[:, :64]], axis=1)
                        w_ref[first + 64 : first + 128, cols] = jnp.concatenate([left[:, 64:], right[:, 64:]], axis=1)
        middle_ref[step] = dot(quads_ref[...], w_ref[...]).astype(jnp.bfloat16)

    @pl.when(step >= 4)
    def _():
        part = step - 4
        width = middle_ref.shape[-1]
        for x in range(4):
            for yl in range(2):
                sx, ys = x, (yl, 2 + yl)
                for core in range(2):
                    first = (x * 4 + yl * 2 + core) * 64
                    for z in range(2):
                        for yh in range(2):
                            lon = 2 * z + yh
                            w2_ref[first : first + 64, lon * 128 : (lon + 1) * 128] = raw_ref[z, core, sx, ys[yh]]
        total = dot(middle_ref[0], w2_ref[:width])
        for chunk in range(1, 4):
            total += dot(middle_ref[chunk], w2_ref[chunk * width : (chunk + 1) * width])
        unpack_decoder(place_ref, (own_ref, other_ref), dec_ref, part)
        kept = (part % 2) * 2 + part // 2
        joined = (normed(total, sgain_ref[...]) + skip_ref[kept]).astype(jnp.bfloat16)
        out_ref[0] = joined


def decode_kernel(x_ref, gain_ref, w_ref, to_win_ref, from_win_ref, out_ref, qkv_ref, mixed_ref):
    step = pl.program_id(0)
    pair, band = step // 2, step % 2
    quarter = BAND // 4
    x = jnp.concatenate([x_ref[part, step].astype(jnp.float32) for part in range(4)], axis=0).astype(jnp.bfloat16)
    x = dot(to_win_ref[...], x)
    h = normed(x, gain_ref[...]).astype(jnp.bfloat16)
    for third in range(3):
        qkv_ref[:, third * C : (third + 1) * C] = dot(h, w_ref[:, third * C : (third + 1) * C]).astype(jnp.bfloat16)
    for window in range(2):
        window_attention(qkv_ref, mixed_ref, window * WIN, None)
    y = dot(mixed_ref[...], w_ref[:, 3 * C :]).astype(jnp.bfloat16)
    first, second = from_windows(from_win_ref, x + y.astype(jnp.float32))
    out_ref[2 * pair, band] = first.astype(jnp.bfloat16)
    out_ref[2 * pair + 1, band] = second.astype(jnp.bfloat16)


def whole(shape):
    return pl.BlockSpec(shape, lambda i: (0,) * len(shape))


PARAMS = pltpu.CompilerParams(vmem_limit_bytes=VMEM_LIMIT)


def encode(band, framed, gain, weights, place):
    to_win = level_windows()
    shape = (LEV, WIN, C)
    out_shapes, out_specs = [jax.ShapeDtypeStruct(shape, jnp.bfloat16)], [whole(shape)]
    if band == 1:
        out_shapes.append(jax.ShapeDtypeStruct((C, 4 * C), jnp.bfloat16))
        out_specs.append(whole((C, 4 * C)))
    return pl.pallas_call(
        functools.partial(encode_kernel, band),
        grid=(2,),
        in_specs=[
            pl.BlockSpec(memory_space=pltpu.SMEM),
            whole(shape),
            whole((1, C)),
            whole((WIN, WIN)),
            whole((WIN, WIN)),
            *[whole(raw.shape) for raw in weights],
        ],
        out_specs=out_specs,
        out_shape=out_shapes,
        scratch_shapes=[pltpu.VMEM((BAND, 3 * C), jnp.bfloat16), pltpu.VMEM((BAND, C), jnp.bfloat16)],
        compiler_params=PARAMS,
        cost_estimate=pl.CostEstimate(flops=2 * 10**9, bytes_accessed=4 * 10**6, transcendentals=700_000),
        name=f"encode_band{band}",
    )(
        place,
        framed.reshape(shape),
        gain.reshape(1, C),
        jnp.asarray(to_win, jnp.bfloat16),
        jnp.asarray(to_win.T, jnp.bfloat16),
        *weights,
    )


def merge_split(encoded, mgain, sgain, raw, dec_raw, place):
    to_merged = merged_from_natural()
    tokens = LEV * ROWS * COLS // 4
    return pl.pallas_call(
        merge_split_kernel,
        grid=(8,),
        in_specs=[
            pl.BlockSpec(memory_space=pltpu.SMEM),
            whole((LEV, 2, WIN, C)),
            whole((1, 4 * C)),
            whole((1, C)),
            pl.BlockSpec((2, 2, 4, 4, 64, 128), lambda i: (i % 4, 0, 0, 0, i // 4, 0)),
            *[pl.BlockSpec((1, 4, 8, 32, 128), lambda i: (jnp.maximum(i - 4, 0), 0, 0, 0, 0))] * 2,
            whole((BAND, BAND)),
        ],
        out_specs=[
            pl.BlockSpec(
                (1, tokens, C),
                lambda i: ((jnp.maximum(i - 4, 0) % 2) * 2 + jnp.maximum(i - 4, 0) // 2, 0, 0),
            ),
            whole((C, 4 * C)),
        ],
        out_shape=[
            jax.ShapeDtypeStruct((4, tokens, C), jnp.bfloat16),
            jax.ShapeDtypeStruct((C, 4 * C), jnp.bfloat16),
        ],
        scratch_shapes=[
            pltpu.VMEM((tokens, 4 * C), jnp.bfloat16),
            pltpu.VMEM((4, tokens, C), jnp.float32),
            pltpu.VMEM((4, tokens, 256), jnp.bfloat16),
            pltpu.VMEM((4 * C, 256), jnp.bfloat16),
            pltpu.VMEM((2 * C, C), jnp.bfloat16),
        ],
        compiler_params=PARAMS,
        name="merge_split",
    )(
        place,
        encoded,
        mgain.reshape(1, 4 * C),
        sgain.reshape(1, C),
        raw,
        *dec_raw,
        jnp.asarray(to_merged, jnp.bfloat16),
    )


def decode(joined, gain, weights):
    to_win = window_from_natural()
    from_merged = to_win @ merged_from_natural().T
    shape = (LEV, 2, WIN, C)
    return pl.pallas_call(
        decode_kernel,
        grid=(4,),
        in_specs=[
            whole((4, 4, BAND // 4, C)),
            whole((1, C)),
            whole((C, 4 * C)),
            whole((BAND, BAND)),
            whole((WIN, WIN)),
        ],
        out_specs=whole(shape),
        out_shape=jax.ShapeDtypeStruct(shape, jnp.bfloat16),
        scratch_shapes=[
            pltpu.VMEM((BAND, 3 * C), jnp.bfloat16),
            pltpu.VMEM((BAND, C), jnp.bfloat16),
        ],
        compiler_params=PARAMS,
        name="decode",
    )(
        joined.reshape(4, 4, BAND // 4, C),
        gain.reshape(1, C),
        weights,
        jnp.asarray(from_merged, jnp.bfloat16),
        jnp.asarray(level_windows().T, jnp.bfloat16),
    )


def passed_along(value, axis, steps):
    if isinstance(axis, str):
        count = lax.axis_size(axis)
        pairs = [(source, (source + steps) % count) for source in range(count)]
    else:
        rows, cols = (lax.axis_size(name) for name in axis)
        pairs = [
            (i * cols + j, ((i + steps) % rows) * cols + (j + steps) % cols) for i in range(rows) for j in range(cols)
        ]
    return lax.ppermute(value, axis, pairs)


def device_index(x, y, z, core):
    return (x * 4 + (y % 2) * 2 + core) * 16 + z * 2 + y // 2


def chips():
    return [(x, y, z, core) for x in range(4) for y in range(4) for z in range(8) for core in range(2)]


def sent(value, to):
    return lax.ppermute(value, ("lat", "lon"), [(device_index(*at), device_index(*to(*at))) for at in chips()])


def from_x(value):
    return [sent(value, lambda x, y, z, c: ((x + steps) % 4, y, z, c)) for steps in (1, 2, 3)]


def from_y(value):
    return [sent(value, lambda x, y, z, c: (x, (y + steps) % 4, z, c)) for steps in (1, 2, 3)]


def from_z(value, steps):
    return sent(value, lambda x, y, z, c: (x, y, (z + steps) % 8, c))


def x_and_y(value):
    groups = [
        [device_index(x, y, z, core) for x in range(4) for y in range(4)] for z in range(8) for core in range(2)
    ]
    blocks = jnp.broadcast_to(value[None], (16,) + value.shape)
    blocks = lax.all_to_all(blocks, ("lat", "lon"), 0, 0, tiled=True, axis_index_groups=groups)
    return blocks.reshape((4, 4) + value.shape)


def z_and_cores(value):
    groups = [
        [device_index(x, y, z, core) for z in range(8) for core in range(2)] for x in range(4) for y in range(4)
    ]
    return lax.all_gather(value, ("lat", "lon"), axis=0, tiled=False, axis_index_groups=groups)


def other_core(value):
    return sent(value, lambda x, y, z, c: (x, y, z, 1 - c))


def together(*values):
    return lax.optimization_barrier(values)


def shards(
    tokens,
    enc_gain,
    enc_qkv,
    enc_proj,
    merge_gain,
    merge_weight,
    split_weight,
    split_gain,
    dec_gain,
    dec_qkv,
    dec_proj,
):
    half_lat = WA // 2
    half_lon = WO // 2
    lat, lon = lax.axis_index("lat"), lax.axis_index("lon")
    last = lat == lax.axis_size("lat") - 1
    place = jnp.stack([lat // 4, (lon % 2) * 2 + (lat // 2) % 2, lon // 2, lat % 2, last.astype(jnp.int32)]).astype(jnp.int32)
    share = jnp.concatenate(
        [jnp.concatenate([enc_qkv, enc_proj], axis=1), jnp.concatenate([dec_qkv, dec_proj], axis=1)], axis=0
    )
    later_share = jnp.concatenate(
        [jnp.concatenate([merge_weight[:64], merge_weight[64:]], axis=1), split_weight], axis=0
    )

    later_share, share = together(later_share, share)
    later = x_and_y(later_share)
    near = [from_z(share, 1), from_z(share, -1)]
    three = jnp.stack([near[0], share, near[1]])
    tokens_sent, three = together(tokens[:, :half_lat], three)
    far, below, later = together(
        [from_z(three, 3), from_z(three[:2], -3)], passed_along(tokens_sent, "lat", -1), later
    )
    later_raw = z_and_cores(later).reshape(8, 2, 4, 4, 128, 128)
    by_z = jnp.concatenate([far[0], three, far[1]], axis=0)
    edge = jnp.concatenate([tokens[:, half_lat:, :half_lon], below[:, :, :half_lon]], axis=1)
    by_y, beyond = together(from_y(by_z), passed_along(edge, "lon", -1))
    by_y = jnp.stack([by_z, *by_y])
    enc_y, dec_y = by_y[:, :, :32], by_y[:, :, 32:]
    framed = [
        jnp.concatenate([tokens[:, half_lat : half_lat + WA, half_lon:], beyond[:, :WA]], axis=2),
        jnp.concatenate(
            [jnp.concatenate([tokens[:, half_lat + WA :], below], axis=1)[:, :, half_lon:], beyond[:, WA:]], axis=2
        ),
    ]
    enc_x, framed = together(from_x(enc_y), framed)
    enc_x = jnp.stack(enc_x)
    enc_raw = [enc_y, enc_x, other_core(enc_y), other_core(enc_x)]
    second, enc_w = encode(1, framed[1], enc_gain, enc_raw, place)
    second = second.reshape(LEV, WA, COLS, C)
    (first,) = encode(0, framed[0], enc_gain, [enc_w], place)
    first = first.reshape(LEV, WA, COLS, C)
    dec_x, first = together(from_x(dec_y), first)
    dec_own = jnp.stack([dec_y, *dec_x])
    dec_raw = [dec_own, other_core(dec_own)]
    cut_r, cut_c = WA - half_lat, COLS - half_lon
    rows = jnp.concatenate([first, second[:, :cut_r]], axis=1)
    left = passed_along(rows[:, :, cut_c:], "lon", 1)
    above = passed_along(second[:, cut_r:, :cut_c], "lat", 1)
    corner = passed_along(second[:, cut_r:, cut_c:], ("lat", "lon"), 1)
    encoded = jnp.concatenate(
        [jnp.concatenate([corner, above], axis=2), jnp.concatenate([left, rows[:, :, :cut_c]], axis=2)], axis=1
    )
    joined, dec_w = merge_split(
        encoded.reshape(LEV, 2, WIN, C), merge_gain, split_gain, later_raw, dec_raw, place
    )
    return decode(joined, dec_gain, dec_w).reshape(LEV, ROWS, COLS, C)


def solution(mesh):
    return jax.shard_map(
        shards,
        mesh=mesh,
        in_specs=(
            P(None, "lat", "lon", None),
            P(),
            P("lat", "lon"),
            P("lat", "lon"),
            P(),
            P("lat", "lon"),
            P("lat", "lon"),
            P(),
            P(),
            P("lat", "lon"),
            P("lat", "lon"),
        ),
        out_specs=P(None, "lat", "lon", None),
        check_vma=False,
    )
```

```python
import functools

import jax
import jax.numpy as jnp
import numpy as np
from jax import lax
from jax.experimental import pallas as pl
from jax.experimental.pallas import tpu as pltpu
from jax.sharding import PartitionSpec as P

HEADS = 8
WL = 2
WA = 6
WO = 12
WIN = WL * WA * WO
C = 512
HD = C // HEADS
LEV = 4
ROWS = 12
COLS = 24
BAND = 2 * WIN
VMEM_LIMIT = 28 * 1024 * 1024

eps = 1e-05
SCALE = float(HD**-0.5 * np.log2(np.e))


def window_from_natural():
    out = np.zeros((BAND, BAND), np.float32)
    for l in range(WL):
        for r in range(WA):
            for c in range(COLS):
                out[(c // WO) * WIN + (l * WA + r) * WO + c % WO, (l * WA + r) * COLS + c] = 1
    return out


def level_windows():
    return window_from_natural().reshape(2, WL, WIN // 2, WL, WIN)[:, 0, :, 0].reshape(WIN, WIN)


def merged_from_natural():
    out = np.zeros((BAND, BAND), np.float32)
    quarter = BAND // 4
    for l in range(WL):
        for r in range(WA):
            for c in range(COLS):
                part = (c % 2) * 2 + r % 2
                out[part * quarter + (l * (WA // 2) + r // 2) * (COLS // 2) + c // 2, (l * WA + r) * COLS + c] = 1
    return out


MERGE_PART = [0, 2, 1, 3]


def normed(values, gain):
    center = jnp.mean(values, axis=-1, keepdims=True)
    centred = values - center
    spread = jnp.mean(centred * centred, axis=-1, keepdims=True)
    return centred * lax.rsqrt(spread + eps) * gain


def dot(a, b):
    return jnp.dot(a, b, preferred_element_type=jnp.float32)


def window_attention(qkv_ref, mixed_ref, first, same):
    lane = lax.broadcasted_iota(jnp.int32, (WIN, 2 * HD), 1)
    low = lane < HD
    rows = pl.ds(first, WIN)
    for pair in range(HEADS // 2):
        at = pair * 2 * HD
        q = qkv_ref[rows, at : at + 2 * HD]
        k = qkv_ref[rows, C + at : C + at + 2 * HD]
        v = qkv_ref[rows, 2 * C + at : 2 * C + at + 2 * HD]
        vo = jnp.concatenate([v, jnp.ones_like(v)], axis=1)
        halves = []
        for half in range(2):
            own = low if half == 0 else ~low
            scores = lax.dot_general(
                jnp.where(own, q, jnp.zeros_like(q)), k, (((1,), (1,)), ((), ())), preferred_element_type=jnp.float32
            )
            scores = scores * SCALE
            if same is not None:
                scores = jnp.where(same, scores, -jnp.inf)
            top = jnp.max(scores, axis=-1, keepdims=True)
            weights = jnp.exp2(scores - top).astype(jnp.bfloat16)
            summed = dot(weights, vo)
            halves.append(summed[:, : 2 * HD] / summed[:, 2 * HD :])
        mixed_ref[rows, at : at + 2 * HD] = jnp.where(low, halves[0], halves[1]).astype(jnp.bfloat16)


def put_attention(w_ref, rows, group, blocks):
    w_ref[rows, group * 384 : (group + 1) * 384] = jnp.concatenate([b[:, :96] for b in blocks], axis=1)
    w_ref[rows, 3 * C + group * 128 : 3 * C + (group + 1) * 128] = jnp.concatenate([b[:, 96:] for b in blocks], axis=1)


def unpack_encoder(place_ref, raws, w_ref):
    px, py, pz, me = (place_ref[i] for i in range(4))
    for side in range(2):
        near, far = raws[2 * side], raws[2 * side + 1]
        core = lax.rem(me + side, 2)
        for slot in range(4):
            x = lax.rem(px - slot + 4, 4)
            raw = near if slot == 0 else far.at[slot - 1]
            for yl in range(2):
                ys = [lax.rem(py - (2 * yh + yl) + 4, 4) for yh in range(2)]
                rows = pl.ds(pl.multiple_of((x * 4 + yl * 2 + core) * 32, 32), 32)
                for group in range(4):
                    blocks = [raw[ys[j % 2], lax.rem(2 * group + j // 2 - pz + 12, 8)] for j in range(4)]
                    put_attention(w_ref, rows, group, blocks)


def unpack_decoder(place_ref, raws, w_ref, slot):
    px, py, pz, me = (place_ref[i] for i in range(4))
    x = lax.rem(px - slot + 4, 4)
    for side in range(2):
        core = lax.rem(me + side, 2)
        for yl in range(2):
            ys = [lax.rem(py - (2 * yh + yl) + 4, 4) for yh in range(2)]
            rows = pl.ds(pl.multiple_of((x * 4 + yl * 2 + core) * 32, 32), 32)
            for group in range(4):
                blocks = [raws[side][0, ys[j % 2], lax.rem(2 * group + j // 2 - pz + 12, 8)] for j in range(4)]
                put_attention(w_ref, rows, group, blocks)


def to_windows(level_ref, first, second):
    first, second = dot(level_ref[...], first), dot(level_ref[...], second)
    half = WIN // 2
    return jnp.concatenate([first[:half], second[:half], first[half:], second[half:]], axis=0)


def from_windows(level_ref, values):
    half = WIN // 2
    first = jnp.concatenate([values[:half], values[WIN : WIN + half]], axis=0).astype(jnp.bfloat16)
    second = jnp.concatenate([values[half:WIN], values[WIN + half :]], axis=0).astype(jnp.bfloat16)
    return dot(level_ref[...], first), dot(level_ref[...], second)


def encode_kernel(band, place_ref, x_ref, gain_ref, to_win_ref, from_win_ref, *refs):
    pair = pl.program_id(0)
    if band == 1:
        *raws, out_ref, w_ref, qkv_ref, mixed_ref = refs

        @pl.when(pair == 0)
        def _():
            unpack_encoder(place_ref, raws, w_ref)
    else:
        w_ref, out_ref, qkv_ref, mixed_ref = refs

    upper, lower = 2 * pair + 1, (2 * pair + 2) % LEV
    x = [x_ref[level].astype(jnp.float32) for level in (upper, lower)]
    h = [normed(level, gain_ref[...]).astype(jnp.bfloat16) for level in x]
    h = to_windows(to_win_ref, *h).astype(jnp.bfloat16)
    for third in range(3):
        qkv_ref[:, third * C : (third + 1) * C] = dot(h, w_ref[:, third * C : (third + 1) * C]).astype(jnp.bfloat16)
    by_level = (pair == 1).astype(jnp.int32)
    by_row = place_ref[4] if band == 1 else 0

    def label(dim):
        index = lax.broadcasted_iota(jnp.int32, (WIN, WIN), dim)
        second = (index >= WIN // 2).astype(jnp.int32)
        inner = index - second * (WIN // 2)
        return by_level * 3 * second + by_row * (inner >= WIN // 4).astype(jnp.int32)

    same = label(0) == label(1)
    for window in range(2):
        window_attention(qkv_ref, mixed_ref, window * WIN, same)
    y = from_windows(from_win_ref, dot(mixed_ref[...], w_ref[:, 3 * C :]))
    out_ref[upper] = (x[0] + y[0]).astype(jnp.bfloat16)
    out_ref[lower] = (x[1] + y[1]).astype(jnp.bfloat16)


def merge_split_kernel(
    place_ref,
    x_ref,
    mgain_ref,
    sgain_ref,
    raw_ref,
    own_ref,
    other_ref,
    to_merged_ref,
    out_ref,
    dec_ref,
    quads_ref,
    skip_ref,
    middle_ref,
    w_ref,
    w2_ref,
):
    step = pl.program_id(0)
    quarter = BAND // 4

    @pl.when(step == 0)
    def _():
        for pair in range(2):
            for band in range(2):
                x = jnp.concatenate([x_ref[2 * pair, band], x_ref[2 * pair + 1, band]], axis=0)
                m = dot(to_merged_ref[...], x)
                at = (pair * 2 + band) * quarter
                for part in range(4):
                    skip_ref[part, at : at + quarter] = m[part * quarter : (part + 1) * quarter]
        parts = [skip_ref[part] for part in range(4)]
        center = sum(jnp.sum(p, axis=-1, keepdims=True) for p in parts) * (1 / (4 * C))
        spread = sum(jnp.sum((p - center) * (p - center), axis=-1, keepdims=True) for p in parts) * (1 / (4 * C))
        scale = lax.rsqrt(spread + eps)
        for part in range(4):
            quads_ref[:, part * C : (part + 1) * C] = (
                (parts[part] - center) * scale * mgain_ref[:, part * C : (part + 1) * C]
            ).astype(jnp.bfloat16)

    @pl.when(step < 4)
    def _():
        for x in range(4):
            for yl in range(2):
                sx, ys = x, (yl, 2 + yl)
                for core in range(2):
                    first = (x * 4 + yl * 2 + core) * 128
                    for z in range(2):
                        left, right = (raw_ref[z, core, sx, y] for y in ys)
                        cols = slice(z * 128, (z + 1) * 128)
                        w_ref[first : first + 64, cols] = jnp.concatenate([left[:, :64], right[:, :64]], axis=1)
                        w_ref[first + 64 : first + 128, cols] = jnp.concatenate([left[:, 64:], right[:, 64:]], axis=1)
        middle_ref[step] = dot(quads_ref[...], w_ref[...]).astype(jnp.bfloat16)

    @pl.when(step >= 4)
    def _():
        part = step - 4
        width = middle_ref.shape[-1]
        for x in range(4):
            for yl in range(2):
                sx, ys = x, (yl, 2 + yl)
                for core in range(2):
                    first = (x * 4 + yl * 2 + core) * 64
                    for z in range(2):
                        for yh in range(2):
                            lon = 2 * z + yh
                            w2_ref[first : first + 64, lon * 128 : (lon + 1) * 128] = raw_ref[z, core, sx, ys[yh]]
        total = dot(middle_ref[0], w2_ref[:width])
        for chunk in range(1, 4):
            total += dot(middle_ref[chunk], w2_ref[chunk * width : (chunk + 1) * width])
        unpack_decoder(place_ref, (own_ref, other_ref), dec_ref, part)
        kept = (part % 2) * 2 + part // 2
        joined = (normed(total, sgain_ref[...]) + skip_ref[kept]).astype(jnp.bfloat16)
        out_ref[0] = joined


def decode_kernel(x_ref, gain_ref, w_ref, to_win_ref, from_win_ref, out_ref, qkv_ref, mixed_ref):
    step = pl.program_id(0)
    pair, band = step // 2, step % 2
    quarter = BAND // 4
    x = jnp.concatenate([x_ref[part, step].astype(jnp.float32) for part in range(4)], axis=0).astype(jnp.bfloat16)
    x = dot(to_win_ref[...], x)
    h = normed(x, gain_ref[...]).astype(jnp.bfloat16)
    for third in range(3):
        qkv_ref[:, third * C : (third + 1) * C] = dot(h, w_ref[:, third * C : (third + 1) * C]).astype(jnp.bfloat16)
    for window in range(2):
        window_attention(qkv_ref, mixed_ref, window * WIN, None)
    y = dot(mixed_ref[...], w_ref[:, 3 * C :]).astype(jnp.bfloat16)
    first, second = from_windows(from_win_ref, x + y.astype(jnp.float32))
    out_ref[2 * pair, band] = first.astype(jnp.bfloat16)
    out_ref[2 * pair + 1, band] = second.astype(jnp.bfloat16)


def whole(shape):
    return pl.BlockSpec(shape, lambda i: (0,) * len(shape))


PARAMS = pltpu.CompilerParams(vmem_limit_bytes=VMEM_LIMIT)


def encode(band, framed, gain, weights, place):
    to_win = level_windows()
    shape = (LEV, WIN, C)
    out_shapes, out_specs = [jax.ShapeDtypeStruct(shape, jnp.bfloat16)], [whole(shape)]
    if band == 1:
        out_shapes.append(jax.ShapeDtypeStruct((C, 4 * C), jnp.bfloat16))
        out_specs.append(whole((C, 4 * C)))
    return pl.pallas_call(
        functools.partial(encode_kernel, band),
        grid=(2,),
        in_specs=[
            pl.BlockSpec(memory_space=pltpu.SMEM),
            whole(shape),
            whole((1, C)),
            whole((WIN, WIN)),
            whole((WIN, WIN)),
            *[whole(raw.shape) for raw in weights],
        ],
        out_specs=out_specs,
        out_shape=out_shapes,
        scratch_shapes=[pltpu.VMEM((BAND, 3 * C), jnp.bfloat16), pltpu.VMEM((BAND, C), jnp.bfloat16)],
        compiler_params=PARAMS,
        cost_estimate=pl.CostEstimate(flops=2 * 10**9, bytes_accessed=4 * 10**6, transcendentals=700_000),
        name=f"encode_band{band}",
    )(
        place,
        framed.reshape(shape),
        gain.reshape(1, C),
        jnp.asarray(to_win, jnp.bfloat16),
        jnp.asarray(to_win.T, jnp.bfloat16),
        *weights,
    )


def merge_split(encoded, mgain, sgain, raw, dec_raw, place):
    to_merged = merged_from_natural()
    tokens = LEV * ROWS * COLS // 4
    return pl.pallas_call(
        merge_split_kernel,
        grid=(8,),
        in_specs=[
            pl.BlockSpec(memory_space=pltpu.SMEM),
            whole((LEV, 2, WIN, C)),
            whole((1, 4 * C)),
            whole((1, C)),
            pl.BlockSpec((2, 2, 4, 4, 64, 128), lambda i: (i % 4, 0, 0, 0, i // 4, 0)),
            *[pl.BlockSpec((1, 4, 8, 32, 128), lambda i: (jnp.maximum(i - 4, 0), 0, 0, 0, 0))] * 2,
            whole((BAND, BAND)),
        ],
        out_specs=[
            pl.BlockSpec(
                (1, tokens, C),
                lambda i: ((jnp.maximum(i - 4, 0) % 2) * 2 + jnp.maximum(i - 4, 0) // 2, 0, 0),
            ),
            whole((C, 4 * C)),
        ],
        out_shape=[
            jax.ShapeDtypeStruct((4, tokens, C), jnp.bfloat16),
            jax.ShapeDtypeStruct((C, 4 * C), jnp.bfloat16),
        ],
        scratch_shapes=[
            pltpu.VMEM((tokens, 4 * C), jnp.bfloat16),
            pltpu.VMEM((4, tokens, C), jnp.float32),
            pltpu.VMEM((4, tokens, 256), jnp.bfloat16),
            pltpu.VMEM((4 * C, 256), jnp.bfloat16),
            pltpu.VMEM((2 * C, C), jnp.bfloat16),
        ],
        compiler_params=PARAMS,
        name="merge_split",
    )(
        place,
        encoded,
        mgain.reshape(1, 4 * C),
        sgain.reshape(1, C),
        raw,
        *dec_raw,
        jnp.asarray(to_merged, jnp.bfloat16),
    )


def decode(joined, gain, weights):
    to_win = window_from_natural()
    from_merged = to_win @ merged_from_natural().T
    shape = (LEV, 2, WIN, C)
    return pl.pallas_call(
        decode_kernel,
        grid=(4,),
        in_specs=[
            whole((4, 4, BAND // 4, C)),
            whole((1, C)),
            whole((C, 4 * C)),
            whole((BAND, BAND)),
            whole((WIN, WIN)),
        ],
        out_specs=whole(shape),
        out_shape=jax.ShapeDtypeStruct(shape, jnp.bfloat16),
        scratch_shapes=[
            pltpu.VMEM((BAND, 3 * C), jnp.bfloat16),
            pltpu.VMEM((BAND, C), jnp.bfloat16),
        ],
        compiler_params=PARAMS,
        name="decode",
    )(
        joined.reshape(4, 4, BAND // 4, C),
        gain.reshape(1, C),
        weights,
        jnp.asarray(from_merged, jnp.bfloat16),
        jnp.asarray(level_windows().T, jnp.bfloat16),
    )


def passed_along(value, axis, steps):
    if isinstance(axis, str):
        count = lax.axis_size(axis)
        pairs = [(source, (source + steps) % count) for source in range(count)]
    else:
        rows, cols = (lax.axis_size(name) for name in axis)
        pairs = [
            (i * cols + j, ((i + steps) % rows) * cols + (j + steps) % cols) for i in range(rows) for j in range(cols)
        ]
    return lax.ppermute(value, axis, pairs)


def device_index(x, y, z, core):
    return (x * 4 + (y % 2) * 2 + core) * 16 + z * 2 + y // 2


def chips():
    return [(x, y, z, core) for x in range(4) for y in range(4) for z in range(8) for core in range(2)]


def sent(value, to):
    return lax.ppermute(value, ("lat", "lon"), [(device_index(*at), device_index(*to(*at))) for at in chips()])


def from_x(value):
    return [sent(value, lambda x, y, z, c: ((x + steps) % 4, y, z, c)) for steps in (1, 2, 3)]


def from_y(value):
    return [sent(value, lambda x, y, z, c: (x, (y + steps) % 4, z, c)) for steps in (1, 2, 3)]


def from_z(value, steps):
    return sent(value, lambda x, y, z, c: (x, y, (z + steps) % 8, c))


def x_and_y(value):
    groups = [
        [device_index(x, y, z, core) for x in range(4) for y in range(4)] for z in range(8) for core in range(2)
    ]
    blocks = jnp.broadcast_to(value[None], (16,) + value.shape)
    blocks = lax.all_to_all(blocks, ("lat", "lon"), 0, 0, tiled=True, axis_index_groups=groups)
    return blocks.reshape((4, 4) + value.shape)


def z_and_cores(value):
    groups = [
        [device_index(x, y, z, core) for z in range(8) for core in range(2)] for x in range(4) for y in range(4)
    ]
    return lax.all_gather(value, ("lat", "lon"), axis=0, tiled=False, axis_index_groups=groups)


def other_core(value):
    return sent(value, lambda x, y, z, c: (x, y, z, 1 - c))


def together(*values):
    return lax.optimization_barrier(values)


def shards(
    tokens,
    enc_gain,
    enc_qkv,
    enc_proj,
    merge_gain,
    merge_weight,
    split_weight,
    split_gain,
    dec_gain,
    dec_qkv,
    dec_proj,
):
    half_lat = WA // 2
    half_lon = WO // 2
    lat, lon = lax.axis_index("lat"), lax.axis_index("lon")
    last = lat == lax.axis_size("lat") - 1
    place = jnp.stack([lat // 4, (lon % 2) * 2 + (lat // 2) % 2, lon // 2, lat % 2, last.astype(jnp.int32)]).astype(jnp.int32)
    share = jnp.concatenate(
        [jnp.concatenate([enc_qkv, enc_proj], axis=1), jnp.concatenate([dec_qkv, dec_proj], axis=1)], axis=0
    )
    later_share = jnp.concatenate(
        [jnp.concatenate([merge_weight[:64], merge_weight[64:]], axis=1), split_weight], axis=0
    )

    later_share, share = together(later_share, share)
    later = x_and_y(later_share)
    near = [from_z(share, 1), from_z(share, -1)]
    three = jnp.stack([near[0], share, near[1]])
    tokens_sent, three = together(tokens[:, :half_lat], three)
    far, below, later = together(
        [from_z(three, 3), from_z(three[:2], -3)], passed_along(tokens_sent, "lat", -1), later
    )
    later_raw = z_and_cores(later).reshape(8, 2, 4, 4, 128, 128)
    by_z = jnp.concatenate([far[0], three, far[1]], axis=0)
    edge = jnp.concatenate([tokens[:, half_lat:, :half_lon], below[:, :, :half_lon]], axis=1)
    by_y, beyond = together(from_y(by_z), passed_along(edge, "lon", -1))
    by_y = jnp.stack([by_z, *by_y])
    enc_y, dec_y = by_y[:, :, :32], by_y[:, :, 32:]
    framed = [
        jnp.concatenate([tokens[:, half_lat : half_lat + WA, half_lon:], beyond[:, :WA]], axis=2),
        jnp.concatenate(
            [jnp.concatenate([tokens[:, half_lat + WA :], below], axis=1)[:, :, half_lon:], beyond[:, WA:]], axis=2
        ),
    ]
    enc_x, framed = together(from_x(enc_y), framed)
    enc_x = jnp.stack(enc_x)
    enc_raw = [enc_y, enc_x, other_core(enc_y), other_core(enc_x)]
    second, enc_w = encode(1, framed[1], enc_gain, enc_raw, place)
    second = second.reshape(LEV, WA, COLS, C)
    (first,) = encode(0, framed[0], enc_gain, [enc_w], place)
    first = first.reshape(LEV, WA, COLS, C)
    dec_x, first = together(from_x(dec_y), first)
    dec_own = jnp.stack([dec_y, *dec_x])
    dec_raw = [dec_own, other_core(dec_own)]
    cut_r, cut_c = WA - half_lat, COLS - half_lon
    rows = jnp.concatenate([first, second[:, :cut_r]], axis=1)
    left = passed_along(rows[:, :, cut_c:], "lon", 1)
    above = passed_along(second[:, cut_r:, :cut_c], "lat", 1)
    corner = passed_along(second[:, cut_r:, cut_c:], ("lat", "lon"), 1)
    encoded = jnp.concatenate(
        [jnp.concatenate([corner, above], axis=2), jnp.concatenate([left, rows[:, :, :cut_c]], axis=2)], axis=1
    )
    joined, dec_w = merge_split(
        encoded.reshape(LEV, 2, WIN, C), merge_gain, split_gain, later_raw, dec_raw, place
    )
    return decode(joined, dec_gain, dec_w).reshape(LEV, ROWS, COLS, C)


def solution(mesh):
    return jax.shard_map(
        shards,
        mesh=mesh,
        in_specs=(
            P(None, "lat", "lon", None),
            P(),
            P("lat", "lon"),
            P("lat", "lon"),
            P(),
            P("lat", "lon"),
            P("lat", "lon"),
            P(),
            P(),
            P("lat", "lon"),
            P("lat", "lon"),
        ),
        out_specs=P(None, "lat", "lon", None),
        check_vma=False,
    )
```
